32 devices in a mesh: groups: 2 (over y), tok: 4 (over z), head: 2 (over x), sub: 2 (over core).
Axes of the slice: x: 2, y: 2, z: 4, core: 2. Of those that a mesh axis runs over, the one named last changes fastest.
Arguments:
- in_tokens: bfloat16 [16384, 768], P(('groups', 'tok', 'sub')), parts along dimension 0, may hold values from -6 to 6
- target_views: int32 [3072], P(('groups', 'tok', 'sub')), parts along dimension 0, may hold values from 0 to 31
- target_rays: int32 [3072], P(('groups', 'tok', 'sub')), parts along dimension 0, may hold values from 0 to 1023
- camera_turn: float32 [64, 9], P('groups'), parts along dimension 0, may hold values from -0.15 to 0.15
- camera_anchor: float32 [64, 3], P('groups'), parts along dimension 0, may hold values from -4 to 4
- pixels_true: bfloat16 [16, 2, 96, 192], P(('groups', 'tok', 'sub'), 'head'), parts along dimension 0, may hold values from 0 to 1
- transient: int32 [16, 2, 96, 64], P(('groups', 'tok', 'sub'), 'head'), parts along dimension 0, may hold values 0 or 1
- query_weight: bfloat16 [768, 384], P(None, 'head'), may hold values from -0.21875 to 0.21875
- key_weight: bfloat16 [768, 384], P(None, 'head'), may hold values from -0.21875 to 0.21875
- value_weight: bfloat16 [768, 384], P(None, 'head'), may hold values from -0.21875 to 0.21875
- rate_weight: bfloat16 [768, 2], P(None, 'head'), may hold values from -0.21875 to 0.21875
- rate_bias: float32 [2], P('head'), may hold values from -1 to 1
- fast_init: bfloat16 [2, 3, 192, 384], P('head'), may hold values from -0.4375 to 0.4375
- out_weight: bfloat16 [384, 768], P('head'), may hold values from -0.3125 to 0.3125
- ray_weight: bfloat16 [384, 768], replicated, may hold values from -0.3125 to 0.3125
- norm_gain: float32 [768], replicated, may hold values from 0.1 to 1.9
- wide_weight: bfloat16 [768, 1536], P(None, 'head'), may hold values from -0.21875 to 0.21875
- narrow_weight: bfloat16 [768, 1536], P(None, 'head'), may hold values from -0.15625 to 0.15625
- decode_gain: float32 [768], replicated, may hold values from 0.1 to 1.9
- decode_weight: bfloat16 [768, 256], replicated, may hold values from -0.21875 to 0.21875
Outputs:
- render: bfloat16 [16, 2, 96, 192], P(('groups', 'tok', 'sub'), 'head'), parts along dimension 0
- grad_decode: float32 [1536, 256], P(('groups', 'tok', 'sub')), parts along dimension 0
- grad_narrow: float32 [1536, 1536], P(('groups', 'tok', 'sub'), 'head'), parts along dimension 0
The draws below stay inside these ranges and needn't reach their ends.
There are 2 independent parts, one for each index of `groups`. The reference program is written for one: setup_inputs(seed, part) draws one part's arguments, and reference() takes and returns one part's arrays. A program takes and returns all parts, laid end to end along the dimension named above; an argument that names none is the same for every part. Nothing has to cross between parts.
Inputs may be any that keep to these rules, and one draw needn't show every extreme that they name: `transient`: 1 marks a pixel to leave out of the loss. `target_views`: index of the target token's camera. `target_rays`: index of the target token's patch, row-major over the image's patches.
All inputs are finite; a program needn't handle non-finite values. No bound on the sum of `transient` on one device may be relied on, other than what follows from the above.
Results may differ from the reference program's by a relative error of at most 0.024.
Values may be sent and summed in bfloat16 or wider, within the bound.
A program may use at most 64 MiB of HBM per device.

```python
import math
import jax
import jax.numpy as jnp
from jax import lax

D = 768
DH = 192
FH = 384
HEADS = 2
MLP_H = 1536
PATCH = 8
PIX = 64
IMG = 256
RAYS = 1024
VIEWS = 32
BLOCKS = 8
IN_TOKENS = 8192
TGT_TOKENS = 1536
TGT_ROWS = 96
N_HEAD = 2


def plant(array, stream_key, smallest, high):
    index_at = [jax.random.randint(jax.random.fold_in(stream_key, axis), (), 0, length) for axis, length in enumerate(array.shape)]
    widest = array.shape.index(max(array.shape))
    beside = index_at[:widest] + [(index_at[widest] + 1) % array.shape[widest]] + index_at[widest + 1:]
    return array.at[tuple(index_at)].set(smallest).at[tuple(beside)].set(high)


def block_levels(key, dims, cuts, least, top_value):
    factor_of, own = 1.0, jax.random.fold_in(key, 6)
    for position, shards_of in cuts:
        draws = jnp.exp(jax.random.uniform(jax.random.fold_in(own, position), (shards_of,), jnp.float32, least / len(cuts), top_value / len(cuts)))
        factor_of = factor_of * jnp.repeat(draws, dims[position] // shards_of).reshape([-1 if axis == position else 1 for axis in range(len(dims))])
    return factor_of


def gaussian(rng, dims, deviation, reach, shards=(), kind=jnp.bfloat16):
    array = deviation * jax.random.normal(rng, dims, jnp.float32)
    if shards:
        array = array * block_levels(rng, dims, shards, -0.22, 0.18)
    return jnp.clip(array, -reach, reach).astype(kind)


def setup_inputs(seed: int = 0, part: int = 0) -> dict:
    key_of = jax.random.split(jax.random.key(seed), 21)
    part_keys = jax.random.split(jax.random.fold_in(key_of[20], part), 21)
    in_tokens = gaussian(part_keys[0], (IN_TOKENS, D), 1.0, 6.0, ((0, 8),))
    target_views = plant(jax.random.randint(part_keys[1], (TGT_TOKENS,), 0, VIEWS), jax.random.fold_in(part_keys[1], 1), 0, VIEWS - 1).astype(jnp.int32)
    target_rays = plant(jax.random.randint(part_keys[2], (TGT_TOKENS,), 0, RAYS), jax.random.fold_in(part_keys[2], 1), 0, RAYS - 1).astype(jnp.int32)
    camera_turn = jnp.clip(jax.random.uniform(part_keys[3], (VIEWS, 9), jnp.float32, -0.15, 0.15), -0.15, 0.15)
    camera_anchor = gaussian(part_keys[4], (VIEWS, 3), 1.0, 4.0, (), jnp.float32)
    pixels_true = jnp.clip(1.0 * jax.random.uniform(part_keys[5], (BLOCKS, N_HEAD, TGT_ROWS, 3 * PIX), jnp.float32) ** block_levels(part_keys[5], (BLOCKS, N_HEAD, TGT_ROWS, 3 * PIX), ((0, 8), (1, 2)), -0.2, 0.2), 0.0, 1.0).astype(jnp.bfloat16)
    transient = plant((jax.random.randint(part_keys[6], (BLOCKS, N_HEAD, TGT_ROWS, PIX), 0, 4) < 1).astype(jnp.int32), jax.random.fold_in(part_keys[6], 1), 0, 1)
    query_weight = gaussian(key_of[7], (D, HEADS * DH), D ** -0.5, 0.21875, ((1, 2),))
    key_weight = gaussian(key_of[8], (D, HEADS * DH), D ** -0.5, 0.21875, ((1, 2),))
    value_weight = gaussian(key_of[9], (D, HEADS * DH), D ** -0.5, 0.21875, ((1, 2),))
    rate_weight = gaussian(key_of[10], (D, HEADS), D ** -0.5, 0.21875, ((1, 2),))
    rate_bias = jnp.clip(jax.random.uniform(key_of[11], (HEADS,), jnp.float32, -1.0, 1.0) * block_levels(key_of[11], (HEADS,), ((0, 2),), -0.4, 0.0), -1.0, 1.0)
    fast_init = gaussian(key_of[12], (HEADS, 3, DH, FH), DH ** -0.5, 0.4375, ((0, 2),))
    out_weight = gaussian(key_of[13], (HEADS * DH, D), (HEADS * DH) ** -0.5, 0.3125, ((0, 2),))
    ray_weight = gaussian(key_of[14], (6 * PIX, D), (6 * PIX) ** -0.5, 0.3125)
    norm_gain = jnp.clip(1.0 + 0.18 * jax.random.normal(key_of[15], (D,), jnp.float32), 0.1, 1.9)
    wide_weight = gaussian(key_of[16], (D, MLP_H), D ** -0.5, 0.21875, ((1, 2),))
    narrow_weight = gaussian(key_of[17], (D, MLP_H), MLP_H ** -0.5, 0.15625, ((1, 2),))
    decode_gain = jnp.clip(1.0 + 0.18 * jax.random.normal(key_of[18], (D,), jnp.float32), 0.1, 1.9)
    decode_weight = gaussian(key_of[19], (D, 4 * PIX), D ** -0.5, 0.21875)
    return dict(in_tokens=in_tokens, target_views=target_views, target_rays=target_rays, camera_turn=camera_turn, camera_anchor=camera_anchor, pixels_true=pixels_true, transient=transient, query_weight=query_weight, key_weight=key_weight, value_weight=value_weight, rate_weight=rate_weight, rate_bias=rate_bias, fast_init=fast_init, out_weight=out_weight, ray_weight=ray_weight, norm_gain=norm_gain, wide_weight=wide_weight, narrow_weight=narrow_weight, decode_gain=decode_gain, decode_weight=decode_weight)


EPSILON = 1e-06
RATE_SCALE = 0.2
BETA_FLOOR = 0.05

def rms_scale(vector):
    return lax.rsqrt(lax.optimization_barrier(jnp.mean(vector * vector, axis=-1, keepdims=True)) + EPSILON)

def silu_grad(activation_in):
    sigmoid_part = jax.nn.sigmoid(activation_in)
    return sigmoid_part * (1.0 + activation_in * (1.0 - sigmoid_part))

def plucker_rays(view_ids, ray_ids, camera_turn, camera_anchor):
    camera_count = camera_turn.shape[0]
    one_hot = view_ids[:, None] == jnp.arange(camera_count, dtype=jnp.int32)[None, :]
    turn_rows = lax.optimization_barrier(jnp.sum(jnp.where(one_hot[:, :, None], camera_turn[None, :, :], 0.0), axis=1))
    anchor_rows = lax.optimization_barrier(jnp.sum(jnp.where(one_hot[:, :, None], camera_anchor[None, :, :], 0.0), axis=1))
    patch_across = IMG // PATCH
    patch_row = ray_ids // patch_across
    patch_col = ray_ids % patch_across
    pixel_index = jnp.arange(PATCH * PATCH, dtype=jnp.int32)
    column_pos = (patch_col[:, None] * PATCH + pixel_index[None, :] % PATCH).astype(jnp.float32) + 0.5
    row_pos = (patch_row[:, None] * PATCH + pixel_index[None, :] // PATCH).astype(jnp.float32) + 0.5
    camera_x = (column_pos - 0.5 * IMG) / IMG
    camera_y = (row_pos - 0.5 * IMG) / IMG
    dir_x = (1.0 + turn_rows[:, 0:1]) * camera_x + turn_rows[:, 1:2] * camera_y + turn_rows[:, 2:3]
    dir_y = turn_rows[:, 3:4] * camera_x + (1.0 + turn_rows[:, 4:5]) * camera_y + turn_rows[:, 5:6]
    dir_z = turn_rows[:, 6:7] * camera_x + turn_rows[:, 7:8] * camera_y + (1.0 + turn_rows[:, 8:9])
    norm_inv = lax.rsqrt(dir_x * dir_x + dir_y * dir_y + dir_z * dir_z)
    dir_x = dir_x * norm_inv
    dir_y = dir_y * norm_inv
    dir_z = dir_z * norm_inv
    anchor_x = anchor_rows[:, 0:1]
    anchor_y = anchor_rows[:, 1:2]
    anchor_z = anchor_rows[:, 2:3]
    moment_x = anchor_y * dir_z - anchor_z * dir_y
    moment_y = anchor_z * dir_x - anchor_x * dir_z
    moment_z = anchor_x * dir_y - anchor_y * dir_x
    return jnp.concatenate([dir_x, dir_y, dir_z, moment_x, moment_y, moment_z], axis=1).astype(jnp.bfloat16)

def fast_gradient(keys_normed, value_rows, rate_rows, weights):
    pre_first = jnp.dot(keys_normed, weights[0], preferred_element_type=jnp.float32)
    pre_third = jnp.dot(keys_normed, weights[1], preferred_element_type=jnp.float32)
    fast_hidden = (jax.nn.silu(pre_first) * pre_third).astype(jnp.bfloat16)
    descent = (-rate_rows[:, None] * value_rows.astype(jnp.float32)).astype(jnp.bfloat16)
    contract_rows = (((0,), (0,)), ((), ()))
    grad_second = lax.dot_general(descent, fast_hidden, contract_rows, preferred_element_type=jnp.float32)
    grad_hidden = jnp.dot(descent, weights[2], preferred_element_type=jnp.float32)
    grad_pre_first = (grad_hidden * pre_third * silu_grad(pre_first)).astype(jnp.bfloat16)
    grad_pre_third = (grad_hidden * jax.nn.silu(pre_first)).astype(jnp.bfloat16)
    grad_first = lax.dot_general(keys_normed, grad_pre_first, contract_rows, preferred_element_type=jnp.float32)
    grad_third = lax.dot_general(keys_normed, grad_pre_third, contract_rows, preferred_element_type=jnp.float32)
    return jnp.stack([grad_first, grad_third, grad_second])

def renormalize(gradient, start_rows):
    start_float = start_rows.astype(jnp.float32)
    moved_rows = start_float - gradient
    restore = jnp.sqrt(lax.optimization_barrier(jnp.mean(start_float * start_float, axis=-1, keepdims=True)) + EPSILON)
    return (moved_rows * rms_scale(moved_rows) * restore).astype(jnp.bfloat16)

def apply_fast(query_rows, weights):
    apply_first = jnp.dot(query_rows, weights[0], preferred_element_type=jnp.float32)
    apply_third = jnp.dot(query_rows, weights[1], preferred_element_type=jnp.float32)
    apply_hidden = (jax.nn.silu(apply_first) * apply_third).astype(jnp.bfloat16)
    contract_last = (((1,), (1,)), ((), ()))
    return lax.dot_general(apply_hidden, weights[2], contract_last, preferred_element_type=jnp.float32).astype(jnp.bfloat16)

def pixel_loss(logits, truth_rows, transient_bits, loss_scale):
    pixel_count = transient_bits.shape[-1]
    row_total = logits.shape[0]
    colors = logits[:, :3 * pixel_count]
    spread_logit = logits[:, 3 * pixel_count:]
    spread = jax.nn.softplus(spread_logit) + BETA_FLOOR
    error_rows = colors.reshape(row_total, pixel_count, 3) - truth_rows.reshape(row_total, pixel_count, 3).astype(jnp.float32)
    squared = lax.optimization_barrier(jnp.sum(error_rows * error_rows, axis=2))
    keep_mask = (1 - transient_bits).astype(jnp.float32)
    inverse = 1.0 / (spread * spread)
    grad_colors = (keep_mask * inverse * loss_scale)[:, :, None] * error_rows
    grad_spread = keep_mask * (1.0 / spread - squared * inverse / spread) * loss_scale * jax.nn.sigmoid(spread_logit)
    grad_logits = jnp.concatenate([grad_colors.reshape(row_total, 3 * pixel_count), grad_spread], axis=1).astype(jnp.bfloat16)
    return (colors.astype(jnp.bfloat16), grad_logits)

def reference(in_tokens, target_views, target_rays, camera_turn, camera_anchor, pixels_true, transient, query_weight, key_weight, value_weight, rate_weight, rate_bias, fast_init, out_weight, ray_weight, norm_gain, wide_weight, narrow_weight, decode_gain, decode_weight):
    keys_raw = jnp.dot(in_tokens, key_weight, preferred_element_type=jnp.float32).reshape(IN_TOKENS, HEADS, DH)
    keys_normed = (keys_raw * rms_scale(keys_raw)).astype(jnp.bfloat16)
    value_rows = jnp.dot(in_tokens, value_weight, preferred_element_type=jnp.float32).astype(jnp.bfloat16).reshape(IN_TOKENS, HEADS, DH)
    rate_logit = jnp.dot(in_tokens, rate_weight, preferred_element_type=jnp.float32) + rate_bias[None, :]
    rate_rows = jax.nn.softplus(rate_logit) * (RATE_SCALE / math.sqrt(IN_TOKENS))
    features = plucker_rays(target_views, target_rays, camera_turn, camera_anchor)
    embedded = jnp.dot(features, ray_weight, preferred_element_type=jnp.float32).astype(jnp.bfloat16)
    query_raw = jnp.dot(embedded, query_weight, preferred_element_type=jnp.float32).reshape(TGT_TOKENS, HEADS, DH)
    queries = (query_raw * rms_scale(query_raw)).astype(jnp.bfloat16)
    head_outputs = []
    for head_index in range(HEADS):
        fast_grads = fast_gradient(keys_normed[:, head_index], value_rows[:, head_index], rate_rows[:, head_index], fast_init[head_index])
        new_weights = renormalize(fast_grads, fast_init[head_index])
        head_outputs.append(apply_fast(queries[:, head_index], new_weights))
    fast_out = jnp.concatenate(head_outputs, axis=1)
    residual = embedded.astype(jnp.float32) + jnp.dot(fast_out, out_weight, preferred_element_type=jnp.float32)
    normed = (residual * rms_scale(residual) * norm_gain).astype(jnp.bfloat16)
    active = jax.nn.gelu(jnp.dot(normed, wide_weight, preferred_element_type=jnp.float32)).astype(jnp.bfloat16)
    contract_last = (((1,), (1,)), ((), ()))
    contract_rows = (((0,), (0,)), ((), ()))
    block_after = residual + lax.dot_general(active, narrow_weight, contract_last, preferred_element_type=jnp.float32)
    after_scale = rms_scale(block_after)
    decoded_in = (block_after * after_scale * decode_gain).astype(jnp.bfloat16)
    logits = jnp.dot(decoded_in, decode_weight, preferred_element_type=jnp.float32)
    loss_scale = 1.0 / (PIX * math.sqrt(TGT_TOKENS))
    render, grad_logits = pixel_loss(logits, pixels_true.reshape(TGT_TOKENS, 3 * PIX), transient.reshape(TGT_TOKENS, PIX), loss_scale)
    grad_decode = lax.dot_general(decoded_in, grad_logits, contract_rows, preferred_element_type=jnp.float32)
    grad_decoded = lax.dot_general(grad_logits, decode_weight, contract_last, preferred_element_type=jnp.float32)
    gained = grad_decoded * decode_gain
    cubed = after_scale * after_scale * after_scale
    grad_after = (after_scale * gained - block_after * cubed * lax.optimization_barrier(jnp.mean(gained * block_after, axis=1, keepdims=True))).astype(jnp.bfloat16)
    grad_narrow = lax.dot_general(grad_after, active, contract_rows, preferred_element_type=jnp.float32)
    return (render.reshape(BLOCKS, N_HEAD, TGT_ROWS, 3 * PIX), grad_decode, grad_narrow)
```

```python
import functools
import math

import jax
import jax.numpy as jnp
from jax import lax
from jax.experimental import pallas as pl
from jax.experimental.pallas import tpu as pltpu
from jax.sharding import PartitionSpec as P

PATCH = 8
IMG = 256


EPSILON = 1e-06
RATE_SCALE = 0.2
BETA_FLOOR = 0.05


def rms_scale(vector):
    return lax.rsqrt(jnp.mean(vector * vector, axis=-1, keepdims=True) + EPSILON)


def silu_grad(activation_in):
    sigmoid_part = jax.nn.sigmoid(activation_in)
    return sigmoid_part * (1.0 + activation_in * (1.0 - sigmoid_part))


def plucker_rays(view_ids, ray_ids, camera_turn, camera_anchor):
    camera_count = camera_turn.shape[0]
    one_hot = view_ids[:, None] == jnp.arange(camera_count, dtype=jnp.int32)[None, :]
    turn_rows = jnp.sum(jnp.where(one_hot[:, :, None], camera_turn[None, :, :], 0.0), axis=1)
    anchor_rows = jnp.sum(jnp.where(one_hot[:, :, None], camera_anchor[None, :, :], 0.0), axis=1)
    patch_across = IMG // PATCH
    patch_row = ray_ids // patch_across
    patch_col = ray_ids % patch_across
    pixel_index = jnp.arange(PATCH * PATCH, dtype=jnp.int32)
    column_pos = (patch_col[:, None] * PATCH + pixel_index[None, :] % PATCH).astype(
        jnp.float32
    ) + 0.5
    row_pos = (patch_row[:, None] * PATCH + pixel_index[None, :] // PATCH).astype(jnp.float32) + 0.5
    camera_x = (column_pos - 0.5 * IMG) / IMG
    camera_y = (row_pos - 0.5 * IMG) / IMG
    dir_x = (1.0 + turn_rows[:, 0:1]) * camera_x + turn_rows[:, 1:2] * camera_y + turn_rows[:, 2:3]
    dir_y = turn_rows[:, 3:4] * camera_x + (1.0 + turn_rows[:, 4:5]) * camera_y + turn_rows[:, 5:6]
    dir_z = turn_rows[:, 6:7] * camera_x + turn_rows[:, 7:8] * camera_y + (1.0 + turn_rows[:, 8:9])
    norm_inv = lax.rsqrt(dir_x * dir_x + dir_y * dir_y + dir_z * dir_z)
    dir_x = dir_x * norm_inv
    dir_y = dir_y * norm_inv
    dir_z = dir_z * norm_inv
    anchor_x = anchor_rows[:, 0:1]
    anchor_y = anchor_rows[:, 1:2]
    anchor_z = anchor_rows[:, 2:3]
    moment_x = anchor_y * dir_z - anchor_z * dir_y
    moment_y = anchor_z * dir_x - anchor_x * dir_z
    moment_z = anchor_x * dir_y - anchor_y * dir_x
    return jnp.concatenate([dir_x, dir_y, dir_z, moment_x, moment_y, moment_z], axis=1).astype(
        jnp.bfloat16
    )


def fast_gradient(keys_normed, value_rows, rate_rows, weights):
    pre_first = jnp.dot(keys_normed, weights[0], preferred_element_type=jnp.float32)
    pre_third = jnp.dot(keys_normed, weights[1], preferred_element_type=jnp.float32)
    fast_hidden = (jax.nn.silu(pre_first) * pre_third).astype(jnp.bfloat16)
    descent = (-rate_rows[:, None] * value_rows.astype(jnp.float32)).astype(jnp.bfloat16)
    contract_rows = (((0,), (0,)), ((), ()))
    grad_second = lax.dot_general(
        descent, fast_hidden, contract_rows, preferred_element_type=jnp.float32
    )
    grad_hidden = jnp.dot(descent, weights[2], preferred_element_type=jnp.float32)
    grad_pre_first = (grad_hidden * pre_third * silu_grad(pre_first)).astype(jnp.bfloat16)
    grad_pre_third = (grad_hidden * jax.nn.silu(pre_first)).astype(jnp.bfloat16)
    grad_first = lax.dot_general(
        keys_normed, grad_pre_first, contract_rows, preferred_element_type=jnp.float32
    )
    grad_third = lax.dot_general(
        keys_normed, grad_pre_third, contract_rows, preferred_element_type=jnp.float32
    )
    return jnp.stack([grad_first, grad_third, grad_second])


def renormalize(gradient, start_rows):
    start_float = start_rows.astype(jnp.float32)
    moved_rows = start_float - gradient
    restore = jnp.sqrt(jnp.mean(start_float * start_float, axis=-1, keepdims=True) + EPSILON)
    return (moved_rows * rms_scale(moved_rows) * restore).astype(jnp.bfloat16)


def apply_fast(query_rows, weights):
    apply_first = jnp.dot(query_rows, weights[0], preferred_element_type=jnp.float32)
    apply_third = jnp.dot(query_rows, weights[1], preferred_element_type=jnp.float32)
    apply_hidden = (jax.nn.silu(apply_first) * apply_third).astype(jnp.bfloat16)
    contract_last = (((1,), (1,)), ((), ()))
    return lax.dot_general(
        apply_hidden, weights[2], contract_last, preferred_element_type=jnp.float32
    ).astype(jnp.bfloat16)


def pixel_loss(logits, truth_rows, transient_bits, loss_scale):
    pixel_count = transient_bits.shape[-1]
    row_total = logits.shape[0]
    colors = logits[:, : 3 * pixel_count]
    spread_logit = logits[:, 3 * pixel_count :]
    spread = jax.nn.softplus(spread_logit) + BETA_FLOOR
    error_rows = colors.reshape(row_total, pixel_count, 3) - truth_rows.reshape(
        row_total, pixel_count, 3
    ).astype(jnp.float32)
    squared = jnp.sum(error_rows * error_rows, axis=2)
    keep_mask = (1 - transient_bits).astype(jnp.float32)
    inverse = 1.0 / (spread * spread)
    grad_colors = (keep_mask * inverse * loss_scale)[:, :, None] * error_rows
    grad_spread = (
        keep_mask
        * (1.0 / spread - squared * inverse / spread)
        * loss_scale
        * jax.nn.sigmoid(spread_logit)
    )
    grad_logits = jnp.concatenate(
        [grad_colors.reshape(row_total, 3 * pixel_count), grad_spread], axis=1
    ).astype(jnp.bfloat16)
    return (colors.astype(jnp.bfloat16), grad_logits)


def on_device(
    in_tokens,
    target_views,
    target_rays,
    camera_turn,
    camera_anchor,
    pixels_true,
    transient,
    query_weight,
    key_weight,
    value_weight,
    rate_weight,
    rate_bias,
    fast_init,
    out_weight,
    ray_weight,
    norm_gain,
    wide_weight,
    narrow_weight,
    decode_gain,
    decode_weight,
):
    token_devices = lax.axis_size("tok") * lax.axis_size("sub")
    in_total = in_tokens.shape[0] * token_devices
    target_total = target_views.shape[0] * token_devices
    contract_last = (((1,), (1,)), ((), ()))
    contract_rows = (((0,), (0,)), ((), ()))
    keys_raw = jnp.dot(in_tokens, key_weight, preferred_element_type=jnp.float32)
    keys_normed = (keys_raw * rms_scale(keys_raw)).astype(jnp.bfloat16)
    value_rows = jnp.dot(in_tokens, value_weight, preferred_element_type=jnp.float32).astype(
        jnp.bfloat16
    )
    rate_logit = jnp.dot(in_tokens, rate_weight, preferred_element_type=jnp.float32) + rate_bias
    rate_rows = jax.nn.softplus(rate_logit[:, 0]) * (RATE_SCALE / math.sqrt(in_total))
    start_weights = fast_init[0]
    local_grads = fast_gradient(keys_normed, value_rows, rate_rows, start_weights)
    owned_share = lax.psum_scatter(local_grads, ("tok", "sub"), scatter_dimension=1, tiled=True)
    row_count = owned_share.shape[1]
    first_row = lax.axis_index(("tok", "sub")) * row_count
    fresh_rows = renormalize(
        owned_share, lax.dynamic_slice_in_dim(start_weights, first_row, row_count, 1)
    )
    new_weights = lax.all_gather(fresh_rows, ("tok", "sub"), axis=1, tiled=True)
    features = plucker_rays(target_views, target_rays, camera_turn, camera_anchor)
    embedded = jnp.dot(features, ray_weight, preferred_element_type=jnp.float32).astype(
        jnp.bfloat16
    )
    query_raw = jnp.dot(embedded, query_weight, preferred_element_type=jnp.float32)
    queries = (query_raw * rms_scale(query_raw)).astype(jnp.bfloat16)
    applied = apply_fast(queries, new_weights)
    head_terms = jnp.dot(applied, out_weight, preferred_element_type=jnp.float32)
    head_rows = pixels_true.shape[2]
    first_token = lax.axis_index("head") * head_rows
    block_sum = lax.psum_scatter(
        head_terms.astype(jnp.bfloat16), "head", scatter_dimension=0, tiled=True
    ).astype(jnp.float32)
    block_resid = (
        lax.dynamic_slice_in_dim(embedded, first_token, head_rows, 0).astype(jnp.float32)
        + block_sum
    )
    block_normed = (block_resid * rms_scale(block_resid) * norm_gain).astype(jnp.bfloat16)
    normed = lax.all_gather(block_normed, "head", axis=0, tiled=True)
    active = jax.nn.gelu(jnp.dot(normed, wide_weight, preferred_element_type=jnp.float32)).astype(
        jnp.bfloat16
    )
    block_mix = lax.psum_scatter(
        lax.dot_general(
            active, narrow_weight, contract_last, preferred_element_type=jnp.float32
        ).astype(jnp.bfloat16),
        "head",
        scatter_dimension=0,
        tiled=True,
    ).astype(jnp.float32)
    block_after = block_resid + block_mix
    after_scale = rms_scale(block_after)
    decoded_in = (block_after * after_scale * decode_gain).astype(jnp.bfloat16)
    logits = jnp.dot(decoded_in, decode_weight, preferred_element_type=jnp.float32)
    loss_scale = 1.0 / (transient.shape[-1] * math.sqrt(target_total))
    render_rows, grad_logits = pixel_loss(logits, pixels_true[0, 0], transient[0, 0], loss_scale)
    grad_decode_local = lax.dot_general(
        decoded_in, grad_logits, contract_rows, preferred_element_type=jnp.float32
    )
    grad_decoded = lax.dot_general(
        grad_logits, decode_weight, contract_last, preferred_element_type=jnp.float32
    )
    gained = grad_decoded * decode_gain
    cubed = after_scale * after_scale * after_scale
    grad_after = (
        after_scale * gained
        - block_after * cubed * jnp.mean(gained * block_after, axis=1, keepdims=True)
    ).astype(jnp.bfloat16)
    grad_narrow_local = lax.dot_general(
        lax.all_gather(grad_after, "head", axis=0, tiled=True),
        active,
        contract_rows,
        preferred_element_type=jnp.float32,
    )
    decode_heads = lax.psum(grad_decode_local.astype(jnp.bfloat16), "head").astype(jnp.float32)
    grad_decode, grad_narrow = (
        lax.psum_scatter(decode_heads, ("tok", "sub"), scatter_dimension=0, tiled=True),
        lax.psum_scatter(grad_narrow_local, ("tok", "sub"), scatter_dimension=0, tiled=True),
    )
    render = render_rows.reshape(1, 1, render_rows.shape[0], render_rows.shape[1])
    return (render, grad_decode, grad_narrow)


CHUNK_PAD = 16
NT = (((1,), (1,)), ((), ()))
TN = (((0,), (0,)), ((), ()))
MESH = pl.DeviceIdType.MESH


def dot(a, b, dims=None):
    if dims is None:
        dims = (((1,), (0,)), ((), ()))
    return lax.dot_general(a, b, dims, preferred_element_type=jnp.float32)


def dot_exact(a, b, dims):
    return lax.dot_general(
        a, b, dims, precision=lax.Precision.HIGHEST, preferred_element_type=jnp.float32
    )


def softplus(x):
    return jnp.maximum(x, 0.0) + jnp.log1p(jnp.exp(-jnp.abs(x)))


def gelu(x):
    return 0.5 * x * (1.0 + jnp.tanh(0.7978845608028654 * (x + 0.044715 * (x * x * x))))


def scene_kernel(
    tok_n,
    rate_scale,
    loss_scale,
    x_ref,
    kw_ref,
    vw_ref,
    rw_ref,
    rb_ref,
    start_ref,
    emb_ref,
    q_ref,
    truth_ref,
    tran_ref,
    ngain_ref,
    dgain_ref,
    outw_hbm,
    wide_hbm,
    narrow_hbm,
    decw_hbm,
    render_ref,
    gdec_ref,
    gnar_ref,
    outw,
    wide,
    narrow,
    decw,
    gacc,
    startf,
    fsb,
    fpr,
    fps,
    frr,
    ag,
    agp,
    hs,
    hr,
    ns,
    nr,
    ms,
    mr,
    gs,
    gr,
    active,
    gat,
    dlf,
    dsb,
    dpr,
    dps,
    drr,
    dx,
    dxr,
    gsb,
    gpr,
    gps,
    grr,
    send_sem,
    recv_sem,
    local_sem,
):
    t = lax.axis_index("tok")
    h = lax.axis_index("head")
    s = lax.axis_index("sub")
    so = 1 - s
    core = {"sub": so}
    side = {"head": 1 - h}

    loads = [
        pltpu.make_async_copy(src, dst, local_sem.at[i])
        for i, (src, dst) in enumerate(
            ((outw_hbm, outw), (wide_hbm, wide), (narrow_hbm, narrow), (decw_hbm, decw))
        )
    ]
    for load in loads:
        load.start()

    def chip(k):
        return lax.rem(t + k, tok_n)

    def source(k):
        return lax.rem(t + tok_n - k, tok_n)

    count = [0]

    def remote(src, dst, where):
        i = count[0]
        count[0] += 1
        return pltpu.make_async_remote_copy(
            src_ref=src,
            dst_ref=dst,
            send_sem=send_sem.at[i],
            recv_sem=recv_sem.at[i],
            device_id=where,
            device_id_type=MESH,
        )

    others = list(range(1, tok_n))
    every = others + [0]

    barrier = pltpu.get_barrier_semaphore()
    for where in [core, side] + [{"tok": chip(k)} for k in others]:
        pl.semaphore_signal(barrier, inc=1, device_id=where, device_id_type=MESH)

    width = start_ref.shape[1]
    depth = start_ref.shape[2]
    gacc[...] = jnp.zeros_like(gacc)
    step_rows = 256
    rate_rows_w = jnp.broadcast_to(rw_ref[...].astype(jnp.float32), (128, rw_ref.shape[1])).astype(
        jnp.bfloat16
    )

    def token_step(i, carry):
        x = x_ref[pl.ds(pl.multiple_of(i * step_rows, step_rows), step_rows), :]
        keys_raw = dot(x, kw_ref[...], NT)
        keys = (keys_raw * rms_scale(keys_raw)).astype(jnp.bfloat16)
        values = dot(x, vw_ref[...], NT).astype(jnp.bfloat16)
        logit = dot(x, rate_rows_w, NT)[:, 0:1] + rb_ref[...]
        rate = softplus(logit) * rate_scale
        descent = (-rate * values.astype(jnp.float32)).astype(jnp.bfloat16)
        pre_first = dot(keys, start_ref[0])
        pre_third = dot(keys, start_ref[1])
        sig = jax.nn.sigmoid(pre_first)
        silu = pre_first * sig
        hidden = (silu * pre_third).astype(jnp.bfloat16)
        grad_hidden = dot(descent, start_ref[2])
        grad_first = (grad_hidden * pre_third * (sig * (1.0 + pre_first * (1.0 - sig)))).astype(
            jnp.bfloat16
        )
        grad_third = (grad_hidden * silu).astype(jnp.bfloat16)
        gacc[0:width] += dot(keys, grad_first, TN)
        gacc[width : 2 * width] += dot(keys, grad_third, TN)
        gacc[2 * width : 3 * width] += dot(descent, hidden, TN)
        return carry

    lax.fori_loop(0, x_ref.shape[0] // step_rows, token_step, 0)
    for m in range(3):
        startf[m * width : (m + 1) * width] = start_ref[m].astype(jnp.float32)

    rows = 3 * width // (2 * tok_n)
    pad = fsb.shape[1] - rows

    def padded(v):
        return jnp.concatenate([v, jnp.zeros((pad, depth), jnp.float32)], axis=0).astype(
            jnp.bfloat16
        )

    def fast_rows(c, sub):
        return pl.ds(pl.multiple_of((c * 2 + sub) * rows, 8), rows)

    pl.semaphore_wait(barrier, 1 + tok_n)

    fast_pair = {}
    for k in every:
        fsb[k] = padded(gacc[fast_rows(chip(k), so)])
        fast_pair[k] = remote(fsb.at[k], fpr.at[k], core)
        fast_pair[k].start()
    fast_chip = {}
    for k in others:
        fast_pair[k].wait_recv()
        fps[k] = padded(gacc[fast_rows(chip(k), s)] + fpr[k][:rows].astype(jnp.float32))
        fast_chip[k] = remote(fps.at[k], frr.at[k], {"tok": chip(k)})
        fast_chip[k].start()
    fast_pair[0].wait_recv()
    gradient = gacc[fast_rows(t, s)] + fpr[0][:rows].astype(jnp.float32)
    for k in others:
        fast_chip[k].wait_recv()
        gradient = gradient + frr[k][:rows].astype(jnp.float32)
    start = startf[fast_rows(t, s)]
    moved = start - gradient
    restore = jnp.sqrt(jnp.mean(start * start, axis=-1, keepdims=True) + EPSILON)
    ag[0] = padded(moved * rms_scale(moved) * restore)

    gather_chip = {k: remote(ag.at[0], ag.at[k], {"tok": chip(k)}) for k in others}
    gather_core = {k: remote(ag.at[k], agp.at[k], core) for k in every}
    for k in others:
        gather_chip[k].start()
    gather_core[0].start()
    for k in others:
        gather_chip[k].wait_recv()
        gather_core[k].start()
        startf[fast_rows(source(k), s)] = ag[k][:rows].astype(jnp.float32)
    startf[fast_rows(t, s)] = ag[0][:rows].astype(jnp.float32)
    for k in every:
        gather_core[k].wait_recv()
        startf[fast_rows(source(k), so)] = agp[k][:rows].astype(jnp.float32)
    fast = [startf[m * width : (m + 1) * width].astype(jnp.bfloat16) for m in range(3)]

    loads[0].wait()

    def head_term(q):
        first = dot(q, fast[0])
        third = dot(q, fast[1])
        hidden = (first * jax.nn.sigmoid(first) * third).astype(jnp.bfloat16)
        out = dot(hidden, fast[2], NT).astype(jnp.bfloat16)
        return dot(out, outw[...])

    hs[...] = head_term(q_ref[1 - h]).astype(jnp.bfloat16)
    head_copy = remote(hs, hr, side)
    head_copy.start()
    own_term = head_term(q_ref[h])
    resid = emb_ref[h].astype(jnp.float32) + own_term
    head_copy.wait_recv()
    resid = resid + hr[...].astype(jnp.float32)
    ns[...] = (resid * rms_scale(resid) * ngain_ref[...]).astype(jnp.bfloat16)
    norm_copy = remote(ns, nr, side)
    norm_copy.start()

    half = ns.shape[0]
    loads[1].wait()
    active[0:half] = gelu(dot(ns[...], wide[...])).astype(jnp.bfloat16)
    loads[2].wait()
    mixed = dot(active[0:half], narrow[...], NT)
    norm_copy.wait_recv()
    active[half : 2 * half] = gelu(dot(nr[...], wide[...])).astype(jnp.bfloat16)
    ms[...] = dot(active[half : 2 * half], narrow[...], NT).astype(jnp.bfloat16)
    mix_copy = remote(ms, mr, side)
    mix_copy.start()
    truth = truth_ref[...].astype(jnp.float32)
    keep = (1 - tran_ref[...]).astype(jnp.float32).T
    pixels = keep.shape[1]
    spot = lax.broadcasted_iota(jnp.int32, (pixels, 3 * pixels), 1) - 3 * (
        lax.broadcasted_iota(jnp.int32, (pixels, 3 * pixels), 0)
    )
    spread_out = jnp.where((spot >= 0) & (spot < 3), 1.0, 0.0).astype(jnp.float32)
    loads[3].wait()
    mix_copy.wait_recv()
    after = resid + (mixed + mr[...].astype(jnp.float32))
    after_scale = rms_scale(after)
    decoded = (after * after_scale * dgain_ref[...]).astype(jnp.bfloat16)
    logits = dot(decoded, decw[...])

    colors = logits[:, : 3 * pixels]
    render_ref[...] = colors.astype(jnp.bfloat16)
    spread_logit = logits[:, 3 * pixels :]
    spread = softplus(spread_logit) + BETA_FLOOR
    error = colors - truth
    squared = dot_exact(error * error, spread_out, NT)
    inverse = 1.0 / (spread * spread)
    weight = dot_exact(keep * inverse * loss_scale, spread_out, (((1,), (0,)), ((), ())))
    grad_spread = (
        keep
        * (1.0 / spread - squared * inverse / spread)
        * loss_scale
        * jax.nn.sigmoid(spread_logit)
    )
    grad_logits = jnp.concatenate([weight * error, grad_spread], axis=1).astype(jnp.bfloat16)
    grad_decoded = dot(grad_logits, decw[...], NT)
    gained = grad_decoded * dgain_ref[...]
    cubed = after_scale * after_scale * after_scale
    gs[...] = (
        after_scale * gained
        - after * cubed * jnp.mean(gained * after, axis=1, keepdims=True)
    ).astype(jnp.bfloat16)
    grad_copy = remote(gs, gr, side)
    grad_copy.start()

    part = gdec_ref.shape[0]

    def part_rows(c, sub):
        return pl.ds(pl.multiple_of((c * 2 + sub) * part, 8), part)

    dlf[...] = dot(decoded, grad_logits, TN)
    dec_pair = {}
    for k in every:
        dsb[k] = dlf[part_rows(chip(k), so)].astype(jnp.bfloat16)
        dec_pair[k] = remote(dsb.at[k], dpr.at[k], core)
        dec_pair[k].start()

    grad_copy.wait_recv()
    both = jnp.concatenate([gs[...].astype(jnp.float32), gr[...].astype(jnp.float32)], axis=0)
    both_t = both.T
    for i in range(2 * tok_n):
        gat[i] = both_t[i * part : (i + 1) * part].astype(jnp.bfloat16)
    nar_pair = {}
    for k in every:
        gsb[k] = dot(gat[chip(k) * 2 + so], active[...]).astype(jnp.bfloat16)
        nar_pair[k] = remote(gsb.at[k], gpr.at[k], core)
        nar_pair[k].start()
    dec_chip = {}
    for k in others:
        dec_pair[k].wait_recv()
        dps[k] = (dlf[part_rows(chip(k), s)] + dpr[k].astype(jnp.float32)).astype(jnp.bfloat16)
        dec_chip[k] = remote(dps.at[k], drr.at[k], {"tok": chip(k)})
        dec_chip[k].start()
    nar_chip = {}
    for k in others:
        mine = dot(gat[chip(k) * 2 + s], active[...])
        nar_pair[k].wait_recv()
        gps[k] = (mine + gpr[k].astype(jnp.float32)).astype(jnp.bfloat16)
        nar_chip[k] = remote(gps.at[k], grr.at[k], {"tok": chip(k)})
        nar_chip[k].start()
    dec_pair[0].wait_recv()
    dec_sum = dlf[part_rows(t, s)] + dpr[0].astype(jnp.float32)
    for k in others:
        dec_chip[k].wait_recv()
        dec_sum = dec_sum + drr[k].astype(jnp.float32)
    dx[...] = dec_sum
    dec_side = remote(dx, dxr, side)
    dec_side.start()
    nar_pair[0].wait_recv()
    gnar_ref[...] = dot(gat[t * 2 + s], active[...]) + gpr[0].astype(jnp.float32)
    dec_side.wait_recv()
    gdec_ref[...] = dec_sum + dxr[...]
    for k in others:
        nar_chip[k].wait_recv()
        gnar_ref[...] += grr[k].astype(jnp.float32)

    for group in (
        fast_pair,
        fast_chip,
        gather_chip,
        gather_core,
        dec_pair,
        nar_pair,
        dec_chip,
        nar_chip,
    ):
        for copy in group.values():
            copy.wait_send()
    for copy in (head_copy, norm_copy, mix_copy, grad_copy, dec_side):
        copy.wait_send()


def on_device_kernel(
    in_tokens,
    target_views,
    target_rays,
    camera_turn,
    camera_anchor,
    pixels_true,
    transient,
    query_weight,
    key_weight,
    value_weight,
    rate_weight,
    rate_bias,
    fast_init,
    out_weight,
    ray_weight,
    norm_gain,
    wide_weight,
    narrow_weight,
    decode_gain,
    decode_weight,
):
    tok_n = lax.axis_size("tok")
    devices = tok_n * lax.axis_size("sub")
    in_total = in_tokens.shape[0] * devices
    target_total = target_views.shape[0] * devices
    features = plucker_rays(target_views, target_rays, camera_turn, camera_anchor)
    embedded = jnp.dot(features, ray_weight, preferred_element_type=jnp.float32).astype(
        jnp.bfloat16
    )
    query_raw = jnp.dot(embedded, query_weight, preferred_element_type=jnp.float32)
    queries = (query_raw * rms_scale(query_raw)).astype(jnp.bfloat16)
    half = pixels_true.shape[2]
    model = in_tokens.shape[1]
    hidden = wide_weight.shape[1]
    width, depth = fast_init.shape[2:]
    fast_rows = -(-(3 * width // devices) // CHUNK_PAD) * CHUNK_PAD
    part = model // devices
    logit_n = decode_weight.shape[1]
    vmem = pl.BlockSpec(memory_space=pltpu.VMEM)
    anywhere = pl.BlockSpec(memory_space=pl.ANY)
    bf16, f32 = jnp.bfloat16, jnp.float32
    fast_buf = pltpu.VMEM((tok_n, fast_rows, depth), bf16)
    row_buf = pltpu.VMEM((half, model), bf16)
    dec_buf = pltpu.VMEM((tok_n, part, logit_n), bf16)
    nar_buf = pltpu.VMEM((tok_n, part, hidden), bf16)
    copies = 4 * tok_n + 4 * (tok_n - 1) + 5
    render, grad_decode, grad_narrow = pl.pallas_call(
        functools.partial(
            scene_kernel,
            tok_n,
            RATE_SCALE / math.sqrt(in_total),
            1.0 / (transient.shape[-1] * math.sqrt(target_total)),
        ),
        out_shape=(
            jax.ShapeDtypeStruct((half, pixels_true.shape[3]), bf16),
            jax.ShapeDtypeStruct((part, logit_n), f32),
            jax.ShapeDtypeStruct((part, hidden), f32),
        ),
        in_specs=[vmem] * 12 + [anywhere] * 4,
        out_specs=(vmem, vmem, vmem),
        scratch_shapes=[
            pltpu.VMEM(out_weight.shape, bf16),
            pltpu.VMEM(wide_weight.shape, bf16),
            pltpu.VMEM(narrow_weight.shape, bf16),
            pltpu.VMEM(decode_weight.shape, bf16),
            pltpu.VMEM((3 * width, depth), f32),
            pltpu.VMEM((3 * width, depth), f32),
        ]
        + [fast_buf] * 6
        + [row_buf] * 8
        + [
            pltpu.VMEM((2 * half, hidden), bf16),
            pltpu.VMEM((devices, part, 2 * half), bf16),
            pltpu.VMEM((model, logit_n), f32),
        ]
        + [dec_buf] * 4
        + [pltpu.VMEM((part, logit_n), f32)] * 2
        + [nar_buf] * 4
        + [
            pltpu.SemaphoreType.DMA((copies,)),
            pltpu.SemaphoreType.DMA((copies,)),
            pltpu.SemaphoreType.DMA((4,)),
        ],
        compiler_params=pltpu.CompilerParams(
            collective_id=0, has_side_effects=True, vmem_limit_bytes=48 * 2**20
        ),
    )(
        in_tokens,
        key_weight.T,
        value_weight.T,
        rate_weight.T,
        rate_bias.reshape(1, 1),
        fast_init[0],
        embedded.reshape(2, half, model),
        queries.reshape(2, half, width),
        pixels_true[0, 0],
        transient[0, 0].T,
        norm_gain.reshape(1, model),
        decode_gain.reshape(1, model),
        out_weight,
        wide_weight,
        narrow_weight,
        decode_weight,
    )
    return (render[None, None], grad_decode, grad_narrow)


def kernel_fits(mesh):
    return mesh.shape["head"] == 2 and mesh.shape["sub"] == 2 and mesh.shape["tok"] in (2, 4)


def solution(mesh):
    in_specs = (
        P(("groups", "tok", "sub"), None),
        P(("groups", "tok", "sub")),
        P(("groups", "tok", "sub")),
        P("groups", None),
        P("groups", None),
        P(("groups", "tok", "sub"), "head", None, None),
        P(("groups", "tok", "sub"), "head", None, None),
        P(None, "head"),
        P(None, "head"),
        P(None, "head"),
        P(None, "head"),
        P("head"),
        P("head", None, None, None),
        P("head", None),
        P(),
        P(),
        P(None, "head"),
        P(None, "head"),
        P(),
        P(),
    )
    out_specs = (
        P(("groups", "tok", "sub"), "head", None, None),
        P(("groups", "tok", "sub"), None),
        P(("groups", "tok", "sub"), "head"),
    )
    body = on_device_kernel if kernel_fits(mesh) else on_device
    return jax.shard_map(
        body, mesh=mesh, in_specs=in_specs, out_specs=out_specs, check_vma=False
    )
```

```python
import functools
import math

import jax
import jax.numpy as jnp
from jax import lax
from jax.experimental import pallas as pl
from jax.experimental.pallas import tpu as pltpu
from jax.sharding import PartitionSpec as P

PATCH = 8
IMG = 256


EPSILON = 1e-06
RATE_SCALE = 0.2
BETA_FLOOR = 0.05


def rms_scale(vector):
    return lax.rsqrt(jnp.mean(vector * vector, axis=-1, keepdims=True) + EPSILON)


def silu_grad(activation_in):
    sigmoid_part = jax.nn.sigmoid(activation_in)
    return sigmoid_part * (1.0 + activation_in * (1.0 - sigmoid_part))


def plucker_rays(view_ids, ray_ids, camera_turn, camera_anchor):
    camera_count = camera_turn.shape[0]
    one_hot = view_ids[:, None] == jnp.arange(camera_count, dtype=jnp.int32)[None, :]
    turn_rows = jnp.sum(jnp.where(one_hot[:, :, None], camera_turn[None, :, :], 0.0), axis=1)
    anchor_rows = jnp.sum(jnp.where(one_hot[:, :, None], camera_anchor[None, :, :], 0.0), axis=1)
    patch_across = IMG // PATCH
    patch_row = ray_ids // patch_across
    patch_col = ray_ids % patch_across
    pixel_index = jnp.arange(PATCH * PATCH, dtype=jnp.int32)
    column_pos = (patch_col[:, None] * PATCH + pixel_index[None, :] % PATCH).astype(
        jnp.float32
    ) + 0.5
    row_pos = (patch_row[:, None] * PATCH + pixel_index[None, :] // PATCH).astype(jnp.float32) + 0.5
    camera_x = (column_pos - 0.5 * IMG) / IMG
    camera_y = (row_pos - 0.5 * IMG) / IMG
    dir_x = (1.0 + turn_rows[:, 0:1]) * camera_x + turn_rows[:, 1:2] * camera_y + turn_rows[:, 2:3]
    dir_y = turn_rows[:, 3:4] * camera_x + (1.0 + turn_rows[:, 4:5]) * camera_y + turn_rows[:, 5:6]
    dir_z = turn_rows[:, 6:7] * camera_x + turn_rows[:, 7:8] * camera_y + (1.0 + turn_rows[:, 8:9])
    norm_inv = lax.rsqrt(dir_x * dir_x + dir_y * dir_y + dir_z * dir_z)
    dir_x = dir_x * norm_inv
    dir_y = dir_y * norm_inv
    dir_z = dir_z * norm_inv
    anchor_x = anchor_rows[:, 0:1]
    anchor_y = anchor_rows[:, 1:2]
    anchor_z = anchor_rows[:, 2:3]
    moment_x = anchor_y * dir_z - anchor_z * dir_y
    moment_y = anchor_z * dir_x - anchor_x * dir_z
    moment_z = anchor_x * dir_y - anchor_y * dir_x
    return jnp.concatenate([dir_x, dir_y, dir_z, moment_x, moment_y, moment_z], axis=1).astype(
        jnp.bfloat16
    )


def fast_gradient(keys_normed, value_rows, rate_rows, weights):
    pre_first = jnp.dot(keys_normed, weights[0], preferred_element_type=jnp.float32)
    pre_third = jnp.dot(keys_normed, weights[1], preferred_element_type=jnp.float32)
    fast_hidden = (jax.nn.silu(pre_first) * pre_third).astype(jnp.bfloat16)
    descent = (-rate_rows[:, None] * value_rows.astype(jnp.float32)).astype(jnp.bfloat16)
    contract_rows = (((0,), (0,)), ((), ()))
    grad_second = lax.dot_general(
        descent, fast_hidden, contract_rows, preferred_element_type=jnp.float32
    )
    grad_hidden = jnp.dot(descent, weights[2], preferred_element_type=jnp.float32)
    grad_pre_first = (grad_hidden * pre_third * silu_grad(pre_first)).astype(jnp.bfloat16)
    grad_pre_third = (grad_hidden * jax.nn.silu(pre_first)).astype(jnp.bfloat16)
    grad_first = lax.dot_general(
        keys_normed, grad_pre_first, contract_rows, preferred_element_type=jnp.float32
    )
    grad_third = lax.dot_general(
        keys_normed, grad_pre_third, contract_rows, preferred_element_type=jnp.float32
    )
    return jnp.stack([grad_first, grad_third, grad_second])


def renormalize(gradient, start_rows):
    start_float = start_rows.astype(jnp.float32)
    moved_rows = start_float - gradient
    restore = jnp.sqrt(jnp.mean(start_float * start_float, axis=-1, keepdims=True) + EPSILON)
    return (moved_rows * rms_scale(moved_rows) * restore).astype(jnp.bfloat16)


def apply_fast(query_rows, weights):
    apply_first = jnp.dot(query_rows, weights[0], preferred_element_type=jnp.float32)
    apply_third = jnp.dot(query_rows, weights[1], preferred_element_type=jnp.float32)
    apply_hidden = (jax.nn.silu(apply_first) * apply_third).astype(jnp.bfloat16)
    contract_last = (((1,), (1,)), ((), ()))
    return lax.dot_general(
        apply_hidden, weights[2], contract_last, preferred_element_type=jnp.float32
    ).astype(jnp.bfloat16)


def pixel_loss(logits, truth_rows, transient_bits, loss_scale):
    pixel_count = transient_bits.shape[-1]
    row_total = logits.shape[0]
    colors = logits[:, : 3 * pixel_count]
    spread_logit = logits[:, 3 * pixel_count :]
    spread = jax.nn.softplus(spread_logit) + BETA_FLOOR
    error_rows = colors.reshape(row_total, pixel_count, 3) - truth_rows.reshape(
        row_total, pixel_count, 3
    ).astype(jnp.float32)
    squared = jnp.sum(error_rows * error_rows, axis=2)
    keep_mask = (1 - transient_bits).astype(jnp.float32)
    inverse = 1.0 / (spread * spread)
    grad_colors = (keep_mask * inverse * loss_scale)[:, :, None] * error_rows
    grad_spread = (
        keep_mask
        * (1.0 / spread - squared * inverse / spread)
        * loss_scale
        * jax.nn.sigmoid(spread_logit)
    )
    grad_logits = jnp.concatenate(
        [grad_colors.reshape(row_total, 3 * pixel_count), grad_spread], axis=1
    ).astype(jnp.bfloat16)
    return (colors.astype(jnp.bfloat16), grad_logits)


def on_device(
    in_tokens,
    target_views,
    target_rays,
    camera_turn,
    camera_anchor,
    pixels_true,
    transient,
    query_weight,
    key_weight,
    value_weight,
    rate_weight,
    rate_bias,
    fast_init,
    out_weight,
    ray_weight,
    norm_gain,
    wide_weight,
    narrow_weight,
    decode_gain,
    decode_weight,
):
    token_devices = lax.axis_size("tok") * lax.axis_size("sub")
    in_total = in_tokens.shape[0] * token_devices
    target_total = target_views.shape[0] * token_devices
    contract_last = (((1,), (1,)), ((), ()))
    contract_rows = (((0,), (0,)), ((), ()))
    keys_raw = jnp.dot(in_tokens, key_weight, preferred_element_type=jnp.float32)
    keys_normed = (keys_raw * rms_scale(keys_raw)).astype(jnp.bfloat16)
    value_rows = jnp.dot(in_tokens, value_weight, preferred_element_type=jnp.float32).astype(
        jnp.bfloat16
    )
    rate_logit = jnp.dot(in_tokens, rate_weight, preferred_element_type=jnp.float32) + rate_bias
    rate_rows = jax.nn.softplus(rate_logit[:, 0]) * (RATE_SCALE / math.sqrt(in_total))
    start_weights = fast_init[0]
    local_grads = fast_gradient(keys_normed, value_rows, rate_rows, start_weights)
    owned_share = lax.psum_scatter(local_grads, ("tok", "sub"), scatter_dimension=1, tiled=True)
    row_count = owned_share.shape[1]
    first_row = lax.axis_index(("tok", "sub")) * row_count
    fresh_rows = renormalize(
        owned_share, lax.dynamic_slice_in_dim(start_weights, first_row, row_count, 1)
    )
    new_weights = lax.all_gather(fresh_rows, ("tok", "sub"), axis=1, tiled=True)
    features = plucker_rays(target_views, target_rays, camera_turn, camera_anchor)
    embedded = jnp.dot(features, ray_weight, preferred_element_type=jnp.float32).astype(
        jnp.bfloat16
    )
    query_raw = jnp.dot(embedded, query_weight, preferred_element_type=jnp.float32)
    queries = (query_raw * rms_scale(query_raw)).astype(jnp.bfloat16)
    applied = apply_fast(queries, new_weights)
    head_terms = jnp.dot(applied, out_weight, preferred_element_type=jnp.float32)
    head_rows = pixels_true.shape[2]
    first_token = lax.axis_index("head") * head_rows
    block_sum = lax.psum_scatter(
        head_terms.astype(jnp.bfloat16), "head", scatter_dimension=0, tiled=True
    ).astype(jnp.float32)
    block_resid = (
        lax.dynamic_slice_in_dim(embedded, first_token, head_rows, 0).astype(jnp.float32)
        + block_sum
    )
    block_normed = (block_resid * rms_scale(block_resid) * norm_gain).astype(jnp.bfloat16)
    normed = lax.all_gather(block_normed, "head", axis=0, tiled=True)
    active = jax.nn.gelu(jnp.dot(normed, wide_weight, preferred_element_type=jnp.float32)).astype(
        jnp.bfloat16
    )
    block_mix = lax.psum_scatter(
        lax.dot_general(
            active, narrow_weight, contract_last, preferred_element_type=jnp.float32
        ).astype(jnp.bfloat16),
        "head",
        scatter_dimension=0,
        tiled=True,
    ).astype(jnp.float32)
    block_after = block_resid + block_mix
    after_scale = rms_scale(block_after)
    decoded_in = (block_after * after_scale * decode_gain).astype(jnp.bfloat16)
    logits = jnp.dot(decoded_in, decode_weight, preferred_element_type=jnp.float32)
    loss_scale = 1.0 / (transient.shape[-1] * math.sqrt(target_total))
    render_rows, grad_logits = pixel_loss(logits, pixels_true[0, 0], transient[0, 0], loss_scale)
    grad_decode_local = lax.dot_general(
        decoded_in, grad_logits, contract_rows, preferred_element_type=jnp.float32
    )
    grad_decoded = lax.dot_general(
        grad_logits, decode_weight, contract_last, preferred_element_type=jnp.float32
    )
    gained = grad_decoded * decode_gain
    cubed = after_scale * after_scale * after_scale
    grad_after = (
        after_scale * gained
        - block_after * cubed * jnp.mean(gained * block_after, axis=1, keepdims=True)
    ).astype(jnp.bfloat16)
    grad_narrow_local = lax.dot_general(
        lax.all_gather(grad_after, "head", axis=0, tiled=True),
        active,
        contract_rows,
        preferred_element_type=jnp.float32,
    )
    decode_heads = lax.psum(grad_decode_local.astype(jnp.bfloat16), "head").astype(jnp.float32)
    grad_decode, grad_narrow = (
        lax.psum_scatter(decode_heads, ("tok", "sub"), scatter_dimension=0, tiled=True),
        lax.psum_scatter(grad_narrow_local, ("tok", "sub"), scatter_dimension=0, tiled=True),
    )
    render = render_rows.reshape(1, 1, render_rows.shape[0], render_rows.shape[1])
    return (render, grad_decode, grad_narrow)


CHUNK_PAD = 16
NT = (((1,), (1,)), ((), ()))
TN = (((0,), (0,)), ((), ()))
MESH = pl.DeviceIdType.MESH


def dot(a, b, dims=None):
    if dims is None:
        dims = (((1,), (0,)), ((), ()))
    return lax.dot_general(a, b, dims, preferred_element_type=jnp.float32)


def dot_exact(a, b, dims):
    return lax.dot_general(
        a, b, dims, precision=lax.Precision.HIGHEST, preferred_element_type=jnp.float32
    )


def softplus(x):
    return jnp.maximum(x, 0.0) + jnp.log1p(jnp.exp(-jnp.abs(x)))


def gelu(x):
    return 0.5 * x * (1.0 + jnp.tanh(0.7978845608028654 * (x + 0.044715 * (x * x * x))))


def scene_kernel(
    tok_n,
    rate_scale,
    loss_scale,
    rb_ref,
    views_ref,
    rays_ref,
    turn_ref,
    anchor_ref,
    rw_ref,
    truth_ref,
    tran_ref,
    ngain_ref,
    dgain_ref,
    x_hbm,
    kw_hbm,
    vw_hbm,
    fast_hbm,
    ray_hbm,
    qw_hbm,
    outw_hbm,
    wide_hbm,
    narrow_hbm,
    decw_hbm,
    render_ref,
    gdec_ref,
    gnar_ref,
    x_ref,
    kw_ref,
    vw_ref,
    start_ref,
    ray_ref,
    qw_ref,
    emb_ref,
    q_ref,
    outw_side,
    wide_side,
    narrow_side,
    act_side,
    outw,
    wide,
    narrow,
    decw,
    gacc,
    startf,
    fsb,
    fpr,
    fps,
    frr,
    ag,
    agp,
    hs,
    hr,
    gs,
    gr,
    active,
    gat,
    dlf,
    dsb,
    dpr,
    dps,
    drr,
    dx,
    dxr,
    gsb,
    gpr,
    gps,
    grr,
    send_sem,
    recv_sem,
    local_sem,
):
    t = lax.axis_index("tok")
    h = lax.axis_index("head")
    s = lax.axis_index("sub")
    so = 1 - s
    core = {"sub": so}
    side = {"head": 1 - h}

    step_rows = 256
    steps = x_hbm.shape[0] // step_rows
    pairs = [(kw_hbm, kw_ref), (fast_hbm, start_ref), (vw_hbm, vw_ref)]
    pairs += [
        (x_hbm.at[pl.ds(i * step_rows, step_rows)], x_ref.at[pl.ds(i * step_rows, step_rows)])
        for i in range(steps)
    ]
    first_loads = len(pairs)
    pairs += [
        (ray_hbm, ray_ref),
        (qw_hbm, qw_ref),
        (outw_hbm, outw),
        (wide_hbm, wide),
        (narrow_hbm, narrow),
        (decw_hbm, decw),
    ]
    loads = [
        pltpu.make_async_copy(src, dst, local_sem.at[i]) for i, (src, dst) in enumerate(pairs)
    ]
    for load in loads:
        load.start()
    ray_load, qw_load, outw_load, wide_load, narrow_load, decw_load = loads[first_loads:]

    def chip(k):
        return lax.rem(t + k, tok_n)

    def source(k):
        return lax.rem(t + tok_n - k, tok_n)

    count = [0]

    def remote(src, dst, where):
        i = count[0]
        count[0] += 1
        return pltpu.make_async_remote_copy(
            src_ref=src,
            dst_ref=dst,
            send_sem=send_sem.at[i],
            recv_sem=recv_sem.at[i],
            device_id=where,
            device_id_type=MESH,
        )

    others = list(range(1, tok_n))
    every = others + [0]

    barrier = pltpu.get_barrier_semaphore()
    for where in [core, side] + [{"tok": chip(k)} for k in others]:
        pl.semaphore_signal(barrier, inc=1, device_id=where, device_id_type=MESH)

    pl.semaphore_wait(barrier, 1 + tok_n)

    def half_rows(ref):
        n = ref.shape[0] // 2
        return ref.at[pl.ds(pl.multiple_of(s * n, n), n)]

    def fetch(hbm, target):
        over = remote(half_rows(hbm), half_rows(target), side)
        share = remote(half_rows(target), half_rows(target), core)
        return over, share

    outw_over, outw_share = fetch(outw_hbm, outw_side)
    wide_over, wide_share = fetch(wide_hbm, wide_side)
    narrow_over, narrow_share = fetch(narrow_hbm, narrow_side)
    outw_over.start()
    wide_over.start()

    width = start_ref.shape[1]
    depth = start_ref.shape[2]
    gacc[...] = jnp.zeros_like(gacc)
    rate_rows_w = jnp.broadcast_to(rw_ref[...].astype(jnp.float32), (128, rw_ref.shape[1])).astype(
        jnp.bfloat16
    )

    def token_step(i, carry):
        x = x_ref[pl.ds(pl.multiple_of(i * step_rows, step_rows), step_rows), :]
        keys_raw = dot(x, kw_ref[...], NT)
        keys = (keys_raw * rms_scale(keys_raw)).astype(jnp.bfloat16)
        values = dot(x, vw_ref[...], NT).astype(jnp.bfloat16)
        logit = dot(x, rate_rows_w, NT)[:, 0:1] + rb_ref[0]
        rate = softplus(logit) * rate_scale
        descent = (-rate * values.astype(jnp.float32)).astype(jnp.bfloat16)
        pre_first = dot(keys, start_ref[0])
        pre_third = dot(keys, start_ref[1])
        sig = jax.nn.sigmoid(pre_first)
        silu = pre_first * sig
        hidden = (silu * pre_third).astype(jnp.bfloat16)
        grad_hidden = dot(descent, start_ref[2])
        grad_first = (grad_hidden * pre_third * (sig * (1.0 + pre_first * (1.0 - sig)))).astype(
            jnp.bfloat16
        )
        grad_third = (grad_hidden * silu).astype(jnp.bfloat16)
        gacc[0:width] += dot(keys, grad_first, TN)
        gacc[width : 2 * width] += dot(keys, grad_third, TN)
        gacc[2 * width : 3 * width] += dot(descent, hidden, TN)
        return carry

    for load in loads[:first_loads]:
        load.wait()
    lax.fori_loop(0, steps, token_step, 0)
    for m in range(3):
        startf[m * width : (m + 1) * width] = start_ref[m].astype(jnp.float32)

    rows = 3 * width // (2 * tok_n)
    pad = fsb.shape[1] - rows

    def padded(v):
        return jnp.concatenate([v, jnp.zeros((pad, depth), jnp.float32)], axis=0).astype(
            jnp.bfloat16
        )

    def fast_rows(c, sub):
        return pl.ds(pl.multiple_of((c * 2 + sub) * rows, 8), rows)

    outw_over.wait_recv()
    outw_share.start()
    narrow_over.start()

    fast_pair = {}
    for k in every:
        fsb[k] = padded(gacc[fast_rows(chip(k), so)])
        fast_pair[k] = remote(fsb.at[k], fpr.at[k], core)
        fast_pair[k].start()
    fast_chip = {}
    for k in others:
        fast_pair[k].wait_recv()
        fps[k] = padded(gacc[fast_rows(chip(k), s)] + fpr[k][:rows].astype(jnp.float32))
        fast_chip[k] = remote(fps.at[k], frr.at[k], {"tok": chip(k)})
        fast_chip[k].start()

    views = views_ref[...][None, :]
    rays = rays_ref[...][None, :]
    cameras = turn_ref.shape[1]
    targets = views.shape[1]
    chosen = jnp.where(
        lax.broadcasted_iota(jnp.int32, (cameras, targets), 0) == views, 1.0, 0.0
    ).astype(jnp.float32)
    plain = (((1,), (0,)), ((), ()))
    across = IMG // PATCH
    table = jnp.concatenate(
        [
            dot_exact(turn_ref[...], chosen, plain),
            dot_exact(anchor_ref[...], chosen, plain),
            jnp.bitwise_and(rays, across - 1).astype(jnp.float32),
            lax.shift_right_logical(rays, across.bit_length() - 1).astype(jnp.float32),
            jnp.zeros((2, targets), jnp.float32),
        ],
        axis=0,
    ).T

    def entry(i):
        return table[:, i : i + 1]

    spots = lax.broadcasted_iota(jnp.int32, (1, PATCH * PATCH), 1)
    spot_x = jnp.bitwise_and(spots, PATCH - 1).astype(jnp.float32)
    spot_y = lax.shift_right_logical(spots, PATCH.bit_length() - 1).astype(jnp.float32)
    camera_x = (entry(12) * PATCH + spot_x + 0.5 - 0.5 * IMG) / IMG
    camera_y = (entry(13) * PATCH + spot_y + 0.5 - 0.5 * IMG) / IMG
    dir_x = (1.0 + entry(0)) * camera_x + entry(1) * camera_y + entry(2)
    dir_y = entry(3) * camera_x + (1.0 + entry(4)) * camera_y + entry(5)
    dir_z = entry(6) * camera_x + entry(7) * camera_y + (1.0 + entry(8))
    norm_inv = lax.rsqrt(dir_x * dir_x + dir_y * dir_y + dir_z * dir_z)
    dir_x = dir_x * norm_inv
    dir_y = dir_y * norm_inv
    dir_z = dir_z * norm_inv
    features = jnp.concatenate(
        [
            dir_x,
            dir_y,
            dir_z,
            entry(10) * dir_z - entry(11) * dir_y,
            entry(11) * dir_x - entry(9) * dir_z,
            entry(9) * dir_y - entry(10) * dir_x,
        ],
        axis=1,
    ).astype(jnp.bfloat16)
    half = emb_ref.shape[1]
    ray_load.wait()
    qw_load.wait()
    embedded = dot(features, ray_ref[...]).astype(jnp.bfloat16)
    query_raw = dot(embedded, qw_ref[...], NT)
    queries = (query_raw * rms_scale(query_raw)).astype(jnp.bfloat16)
    for i in range(2):
        emb_ref[i] = embedded[i * half : (i + 1) * half]
        q_ref[i] = queries[i * half : (i + 1) * half]

    fast_pair[0].wait_recv()
    gradient = gacc[fast_rows(t, s)] + fpr[0][:rows].astype(jnp.float32)
    for k in others:
        fast_chip[k].wait_recv()
        gradient = gradient + frr[k][:rows].astype(jnp.float32)
    start = startf[fast_rows(t, s)]
    moved = start - gradient
    restore = jnp.sqrt(jnp.mean(start * start, axis=-1, keepdims=True) + EPSILON)
    ag[0] = padded(moved * rms_scale(moved) * restore)

    gather_chip = {k: remote(ag.at[0], ag.at[k], {"tok": chip(k)}) for k in others}
    gather_core = {k: remote(ag.at[k], agp.at[k], core) for k in every}
    for k in others:
        gather_chip[k].start()
    gather_core[0].start()
    wide_over.wait_recv()
    wide_share.start()
    for k in others:
        gather_chip[k].wait_recv()
        gather_core[k].start()
        startf[fast_rows(source(k), s)] = ag[k][:rows].astype(jnp.float32)
    startf[fast_rows(t, s)] = ag[0][:rows].astype(jnp.float32)
    for k in every:
        gather_core[k].wait_recv()
        startf[fast_rows(source(k), so)] = agp[k][:rows].astype(jnp.float32)
    fast = [startf[m * width : (m + 1) * width].astype(jnp.bfloat16) for m in range(3)]

    def head_out(q):
        first = dot(q, fast[0])
        third = dot(q, fast[1])
        hidden = (first * jax.nn.sigmoid(first) * third).astype(jnp.bfloat16)
        return dot(hidden, fast[2], NT).astype(jnp.bfloat16)

    hs[...] = head_out(q_ref[1 - h])
    head_copy = remote(hs, hr, side)
    head_copy.start()
    own_out = head_out(q_ref[h])
    outw_load.wait()
    outw_share.wait_recv()
    resid = emb_ref[h].astype(jnp.float32) + dot(own_out, outw[...])
    narrow_over.wait_recv()
    narrow_share.start()
    head_copy.wait_recv()
    resid = resid + dot(hr[...], outw_side[...])
    normed = (resid * rms_scale(resid) * ngain_ref[...][None, :]).astype(jnp.bfloat16)

    wide_load.wait()
    wide_share.wait_recv()
    act_side[...] = gelu(dot(normed, wide_side[...])).astype(jnp.bfloat16)
    act_copy = remote(act_side, active.at[pl.ds(half, half)], side)
    act_copy.start()
    active[0:half] = gelu(dot(normed, wide[...])).astype(jnp.bfloat16)
    narrow_load.wait()
    mixed = dot(active[0:half], narrow[...], NT)
    narrow_share.wait_recv()
    after = resid + (mixed + dot(act_side[...], narrow_side[...], NT))
    truth = truth_ref[...].astype(jnp.float32)
    keep = (1 - tran_ref[...]).astype(jnp.float32).T
    pixels = keep.shape[1]
    spot = lax.broadcasted_iota(jnp.int32, (pixels, 3 * pixels), 1) - 3 * (
        lax.broadcasted_iota(jnp.int32, (pixels, 3 * pixels), 0)
    )
    spread_out = jnp.where((spot >= 0) & (spot < 3), 1.0, 0.0).astype(jnp.float32)
    decw_load.wait()
    after_scale = rms_scale(after)
    decoded = (after * after_scale * dgain_ref[...][None, :]).astype(jnp.bfloat16)
    logits = dot(decoded, decw[...])

    colors = logits[:, : 3 * pixels]
    render_ref[...] = colors.astype(jnp.bfloat16)
    spread_logit = logits[:, 3 * pixels :]
    spread = softplus(spread_logit) + BETA_FLOOR
    error = colors - truth
    squared = dot_exact(error * error, spread_out, NT)
    inverse = 1.0 / (spread * spread)
    weight = dot_exact(keep * inverse * loss_scale, spread_out, (((1,), (0,)), ((), ())))
    grad_spread = (
        keep
        * (1.0 / spread - squared * inverse / spread)
        * loss_scale
        * jax.nn.sigmoid(spread_logit)
    )
    grad_logits = jnp.concatenate([weight * error, grad_spread], axis=1).astype(jnp.bfloat16)
    grad_decoded = dot(grad_logits, decw[...], NT)
    gained = grad_decoded * dgain_ref[...][None, :]
    cubed = after_scale * after_scale * after_scale
    gs[...] = (
        after_scale * gained
        - after * cubed * jnp.mean(gained * after, axis=1, keepdims=True)
    ).astype(jnp.bfloat16)
    grad_copy = remote(gs, gr, side)
    grad_copy.start()

    part = gdec_ref.shape[0]

    def part_rows(c, sub):
        return pl.ds(pl.multiple_of((c * 2 + sub) * part, 8), part)

    dlf[...] = dot(decoded, grad_logits, TN)
    dec_pair = {}
    for k in every:
        dsb[k] = dlf[part_rows(chip(k), so)].astype(jnp.bfloat16)
        dec_pair[k] = remote(dsb.at[k], dpr.at[k], core)
        dec_pair[k].start()

    grad_copy.wait_recv()
    act_copy.wait_recv()
    both = jnp.concatenate([gs[...].astype(jnp.float32), gr[...].astype(jnp.float32)], axis=0)
    both_t = both.T
    for i in range(2 * tok_n):
        gat[i] = both_t[i * part : (i + 1) * part].astype(jnp.bfloat16)
    nar_pair = {}
    for k in every:
        gsb[k] = dot(gat[chip(k) * 2 + so], active[...]).astype(jnp.bfloat16)
        nar_pair[k] = remote(gsb.at[k], gpr.at[k], core)
        nar_pair[k].start()
    dec_chip = {}
    for k in others:
        dec_pair[k].wait_recv()
        dps[k] = (dlf[part_rows(chip(k), s)] + dpr[k].astype(jnp.float32)).astype(jnp.bfloat16)
        dec_chip[k] = remote(dps.at[k], drr.at[k], {"tok": chip(k)})
        dec_chip[k].start()
    nar_chip = {}
    for k in others:
        mine = dot(gat[chip(k) * 2 + s], active[...])
        nar_pair[k].wait_recv()
        gps[k] = (mine + gpr[k].astype(jnp.float32)).astype(jnp.bfloat16)
        nar_chip[k] = remote(gps.at[k], grr.at[k], {"tok": chip(k)})
        nar_chip[k].start()
    dec_pair[0].wait_recv()
    dec_sum = dlf[part_rows(t, s)] + dpr[0].astype(jnp.float32)
    for k in others:
        dec_chip[k].wait_recv()
        dec_sum = dec_sum + drr[k].astype(jnp.float32)
    dx[...] = dec_sum
    dec_side = remote(dx, dxr, side)
    dec_side.start()
    nar_pair[0].wait_recv()
    gnar_ref[...] = dot(gat[t * 2 + s], active[...]) + gpr[0].astype(jnp.float32)
    dec_side.wait_recv()
    gdec_ref[...] = dec_sum + dxr[...]
    for k in others:
        nar_chip[k].wait_recv()
        gnar_ref[...] += grr[k].astype(jnp.float32)

    for group in (
        fast_pair,
        fast_chip,
        gather_chip,
        gather_core,
        dec_pair,
        nar_pair,
        dec_chip,
        nar_chip,
    ):
        for copy in group.values():
            copy.wait_send()
    for copy in (
        head_copy,
        act_copy,
        grad_copy,
        dec_side,
        outw_over,
        outw_share,
        wide_over,
        wide_share,
        narrow_over,
        narrow_share,
    ):
        copy.wait_send()


def on_device_kernel(
    in_tokens,
    target_views,
    target_rays,
    camera_turn,
    camera_anchor,
    pixels_true,
    transient,
    query_weight,
    key_weight,
    value_weight,
    rate_weight,
    rate_bias,
    fast_init,
    out_weight,
    ray_weight,
    norm_gain,
    wide_weight,
    narrow_weight,
    decode_gain,
    decode_weight,
):
    tok_n = lax.axis_size("tok")
    devices = tok_n * lax.axis_size("sub")
    in_total = in_tokens.shape[0] * devices
    target_total = target_views.shape[0] * devices
    half = pixels_true.shape[2]
    model = in_tokens.shape[1]
    hidden = wide_weight.shape[1]
    width, depth = fast_init.shape[2:]
    fast_rows = -(-(3 * width // devices) // CHUNK_PAD) * CHUNK_PAD
    part = model // devices
    logit_n = decode_weight.shape[1]
    vmem = pl.BlockSpec(memory_space=pltpu.VMEM)
    anywhere = pl.BlockSpec(memory_space=pl.ANY)
    bf16, f32 = jnp.bfloat16, jnp.float32
    fast_buf = pltpu.VMEM((tok_n, fast_rows, depth), bf16)
    row_buf = pltpu.VMEM((half, model), bf16)
    dec_buf = pltpu.VMEM((tok_n, part, logit_n), bf16)
    nar_buf = pltpu.VMEM((tok_n, part, hidden), bf16)
    copies = 4 * tok_n + 4 * (tok_n - 1) + 10
    render, grad_decode, grad_narrow = pl.pallas_call(
        functools.partial(
            scene_kernel,
            tok_n,
            RATE_SCALE / math.sqrt(in_total),
            1.0 / (transient.shape[-1] * math.sqrt(target_total)),
        ),
        out_shape=(
            jax.ShapeDtypeStruct((half, pixels_true.shape[3]), bf16),
            jax.ShapeDtypeStruct((part, logit_n), f32),
            jax.ShapeDtypeStruct((part, hidden), f32),
        ),
        in_specs=[pl.BlockSpec(memory_space=pltpu.SMEM)] + [vmem] * 9 + [anywhere] * 10,
        out_specs=(vmem, vmem, vmem),
        scratch_shapes=[
            pltpu.VMEM(in_tokens.shape, bf16),
            pltpu.VMEM((width, model), bf16),
            pltpu.VMEM((width, model), bf16),
            pltpu.VMEM((3, width, depth), bf16),
            pltpu.VMEM(ray_weight.shape, bf16),
            pltpu.VMEM((width, model), bf16),
            pltpu.VMEM((2, half, model), bf16),
            pltpu.VMEM((2, half, width), bf16),
            pltpu.VMEM(out_weight.shape, bf16),
            pltpu.VMEM(wide_weight.shape, bf16),
            pltpu.VMEM(narrow_weight.shape, bf16),
            pltpu.VMEM((half, hidden), bf16),
            pltpu.VMEM(out_weight.shape, bf16),
            pltpu.VMEM(wide_weight.shape, bf16),
            pltpu.VMEM(narrow_weight.shape, bf16),
            pltpu.VMEM(decode_weight.shape, bf16),
            pltpu.VMEM((3 * width, depth), f32),
            pltpu.VMEM((3 * width, depth), f32),
        ]
        + [fast_buf] * 6
        + [pltpu.VMEM((half, width), bf16)] * 2
        + [row_buf] * 2
        + [
            pltpu.VMEM((2 * half, hidden), bf16),
            pltpu.VMEM((devices, part, 2 * half), bf16),
            pltpu.VMEM((model, logit_n), f32),
        ]
        + [dec_buf] * 4
        + [pltpu.VMEM((part, logit_n), f32)] * 2
        + [nar_buf] * 4
        + [
            pltpu.SemaphoreType.DMA((copies,)),
            pltpu.SemaphoreType.DMA((copies,)),
            pltpu.SemaphoreType.DMA((9 + in_tokens.shape[0] // 256,)),
        ],
        compiler_params=pltpu.CompilerParams(
            collective_id=0, has_side_effects=True, vmem_limit_bytes=60 * 2**20
        ),
    )(
        rate_bias,
        target_views,
        target_rays,
        camera_turn.T,
        camera_anchor.T,
        rate_weight.T,
        pixels_true[0, 0],
        transient[0, 0].T,
        norm_gain,
        decode_gain,
        in_tokens,
        key_weight.T,
        value_weight.T,
        fast_init[0],
        ray_weight,
        query_weight.T,
        out_weight,
        wide_weight,
        narrow_weight,
        decode_weight,
    )
    return (render[None, None], grad_decode, grad_narrow)


def kernel_fits(mesh):
    return mesh.shape["head"] == 2 and mesh.shape["sub"] == 2 and mesh.shape["tok"] in (2, 4)


def solution(mesh):
    in_specs = (
        P(("groups", "tok", "sub"), None),
        P(("groups", "tok", "sub")),
        P(("groups", "tok", "sub")),
        P("groups", None),
        P("groups", None),
        P(("groups", "tok", "sub"), "head", None, None),
        P(("groups", "tok", "sub"), "head", None, None),
        P(None, "head"),
        P(None, "head"),
        P(None, "head"),
        P(None, "head"),
        P("head"),
        P("head", None, None, None),
        P("head", None),
        P(),
        P(),
        P(None, "head"),
        P(None, "head"),
        P(),
        P(),
    )
    out_specs = (
        P(("groups", "tok", "sub"), "head", None, None),
        P(("groups", "tok", "sub"), None),
        P(("groups", "tok", "sub"), "head"),
    )
    body = on_device_kernel if kernel_fits(mesh) else on_device
    return jax.shard_map(
        body, mesh=mesh, in_specs=in_specs, out_specs=out_specs, check_vma=False
    )
```

```python
import functools
import math

import jax
import jax.numpy as jnp
from jax import lax
from jax.experimental import pallas as pl
from jax.experimental.pallas import tpu as pltpu
from jax.sharding import PartitionSpec as P

PATCH = 8
IMG = 256


EPSILON = 1e-06
RATE_SCALE = 0.2
BETA_FLOOR = 0.05


def rms_scale(vector):
    return lax.rsqrt(jnp.mean(vector * vector, axis=-1, keepdims=True) + EPSILON)


def silu_grad(activation_in):
    sigmoid_part = jax.nn.sigmoid(activation_in)
    return sigmoid_part * (1.0 + activation_in * (1.0 - sigmoid_part))


def plucker_rays(view_ids, ray_ids, camera_turn, camera_anchor):
    camera_count = camera_turn.shape[0]
    one_hot = view_ids[:, None] == jnp.arange(camera_count, dtype=jnp.int32)[None, :]
    turn_rows = jnp.sum(jnp.where(one_hot[:, :, None], camera_turn[None, :, :], 0.0), axis=1)
    anchor_rows = jnp.sum(jnp.where(one_hot[:, :, None], camera_anchor[None, :, :], 0.0), axis=1)
    patch_across = IMG // PATCH
    patch_row = ray_ids // patch_across
    patch_col = ray_ids % patch_across
    pixel_index = jnp.arange(PATCH * PATCH, dtype=jnp.int32)
    column_pos = (patch_col[:, None] * PATCH + pixel_index[None, :] % PATCH).astype(
        jnp.float32
    ) + 0.5
    row_pos = (patch_row[:, None] * PATCH + pixel_index[None, :] // PATCH).astype(jnp.float32) + 0.5
    camera_x = (column_pos - 0.5 * IMG) / IMG
    camera_y = (row_pos - 0.5 * IMG) / IMG
    dir_x = (1.0 + turn_rows[:, 0:1]) * camera_x + turn_rows[:, 1:2] * camera_y + turn_rows[:, 2:3]
    dir_y = turn_rows[:, 3:4] * camera_x + (1.0 + turn_rows[:, 4:5]) * camera_y + turn_rows[:, 5:6]
    dir_z = turn_rows[:, 6:7] * camera_x + turn_rows[:, 7:8] * camera_y + (1.0 + turn_rows[:, 8:9])
    norm_inv = lax.rsqrt(dir_x * dir_x + dir_y * dir_y + dir_z * dir_z)
    dir_x = dir_x * norm_inv
    dir_y = dir_y * norm_inv
    dir_z = dir_z * norm_inv
    anchor_x = anchor_rows[:, 0:1]
    anchor_y = anchor_rows[:, 1:2]
    anchor_z = anchor_rows[:, 2:3]
    moment_x = anchor_y * dir_z - anchor_z * dir_y
    moment_y = anchor_z * dir_x - anchor_x * dir_z
    moment_z = anchor_x * dir_y - anchor_y * dir_x
    return jnp.concatenate([dir_x, dir_y, dir_z, moment_x, moment_y, moment_z], axis=1).astype(
        jnp.bfloat16
    )


def fast_gradient(keys_normed, value_rows, rate_rows, weights):
    pre_first = jnp.dot(keys_normed, weights[0], preferred_element_type=jnp.float32)
    pre_third = jnp.dot(keys_normed, weights[1], preferred_element_type=jnp.float32)
    fast_hidden = (jax.nn.silu(pre_first) * pre_third).astype(jnp.bfloat16)
    descent = (-rate_rows[:, None] * value_rows.astype(jnp.float32)).astype(jnp.bfloat16)
    contract_rows = (((0,), (0,)), ((), ()))
    grad_second = lax.dot_general(
        descent, fast_hidden, contract_rows, preferred_element_type=jnp.float32
    )
    grad_hidden = jnp.dot(descent, weights[2], preferred_element_type=jnp.float32)
    grad_pre_first = (grad_hidden * pre_third * silu_grad(pre_first)).astype(jnp.bfloat16)
    grad_pre_third = (grad_hidden * jax.nn.silu(pre_first)).astype(jnp.bfloat16)
    grad_first = lax.dot_general(
        keys_normed, grad_pre_first, contract_rows, preferred_element_type=jnp.float32
    )
    grad_third = lax.dot_general(
        keys_normed, grad_pre_third, contract_rows, preferred_element_type=jnp.float32
    )
    return jnp.stack([grad_first, grad_third, grad_second])


def renormalize(gradient, start_rows):
    start_float = start_rows.astype(jnp.float32)
    moved_rows = start_float - gradient
    restore = jnp.sqrt(jnp.mean(start_float * start_float, axis=-1, keepdims=True) + EPSILON)
    return (moved_rows * rms_scale(moved_rows) * restore).astype(jnp.bfloat16)


def apply_fast(query_rows, weights):
    apply_first = jnp.dot(query_rows, weights[0], preferred_element_type=jnp.float32)
    apply_third = jnp.dot(query_rows, weights[1], preferred_element_type=jnp.float32)
    apply_hidden = (jax.nn.silu(apply_first) * apply_third).astype(jnp.bfloat16)
    contract_last = (((1,), (1,)), ((), ()))
    return lax.dot_general(
        apply_hidden, weights[2], contract_last, preferred_element_type=jnp.float32
    ).astype(jnp.bfloat16)


def pixel_loss(logits, truth_rows, transient_bits, loss_scale):
    pixel_count = transient_bits.shape[-1]
    row_total = logits.shape[0]
    colors = logits[:, : 3 * pixel_count]
    spread_logit = logits[:, 3 * pixel_count :]
    spread = jax.nn.softplus(spread_logit) + BETA_FLOOR
    error_rows = colors.reshape(row_total, pixel_count, 3) - truth_rows.reshape(
        row_total, pixel_count, 3
    ).astype(jnp.float32)
    squared = jnp.sum(error_rows * error_rows, axis=2)
    keep_mask = (1 - transient_bits).astype(jnp.float32)
    inverse = 1.0 / (spread * spread)
    grad_colors = (keep_mask * inverse * loss_scale)[:, :, None] * error_rows
    grad_spread = (
        keep_mask
        * (1.0 / spread - squared * inverse / spread)
        * loss_scale
        * jax.nn.sigmoid(spread_logit)
    )
    grad_logits = jnp.concatenate(
        [grad_colors.reshape(row_total, 3 * pixel_count), grad_spread], axis=1
    ).astype(jnp.bfloat16)
    return (colors.astype(jnp.bfloat16), grad_logits)


def on_device(
    in_tokens,
    target_views,
    target_rays,
    camera_turn,
    camera_anchor,
    pixels_true,
    transient,
    query_weight,
    key_weight,
    value_weight,
    rate_weight,
    rate_bias,
    fast_init,
    out_weight,
    ray_weight,
    norm_gain,
    wide_weight,
    narrow_weight,
    decode_gain,
    decode_weight,
):
    token_devices = lax.axis_size("tok") * lax.axis_size("sub")
    in_total = in_tokens.shape[0] * token_devices
    target_total = target_views.shape[0] * token_devices
    contract_last = (((1,), (1,)), ((), ()))
    contract_rows = (((0,), (0,)), ((), ()))
    keys_raw = jnp.dot(in_tokens, key_weight, preferred_element_type=jnp.float32)
    keys_normed = (keys_raw * rms_scale(keys_raw)).astype(jnp.bfloat16)
    value_rows = jnp.dot(in_tokens, value_weight, preferred_element_type=jnp.float32).astype(
        jnp.bfloat16
    )
    rate_logit = jnp.dot(in_tokens, rate_weight, preferred_element_type=jnp.float32) + rate_bias
    rate_rows = jax.nn.softplus(rate_logit[:, 0]) * (RATE_SCALE / math.sqrt(in_total))
    start_weights = fast_init[0]
    local_grads = fast_gradient(keys_normed, value_rows, rate_rows, start_weights)
    owned_share = lax.psum_scatter(local_grads, ("tok", "sub"), scatter_dimension=1, tiled=True)
    row_count = owned_share.shape[1]
    first_row = lax.axis_index(("tok", "sub")) * row_count
    fresh_rows = renormalize(
        owned_share, lax.dynamic_slice_in_dim(start_weights, first_row, row_count, 1)
    )
    new_weights = lax.all_gather(fresh_rows, ("tok", "sub"), axis=1, tiled=True)
    features = plucker_rays(target_views, target_rays, camera_turn, camera_anchor)
    embedded = jnp.dot(features, ray_weight, preferred_element_type=jnp.float32).astype(
        jnp.bfloat16
    )
    query_raw = jnp.dot(embedded, query_weight, preferred_element_type=jnp.float32)
    queries = (query_raw * rms_scale(query_raw)).astype(jnp.bfloat16)
    applied = apply_fast(queries, new_weights)
    head_terms = jnp.dot(applied, out_weight, preferred_element_type=jnp.float32)
    head_rows = pixels_true.shape[2]
    first_token = lax.axis_index("head") * head_rows
    block_sum = lax.psum_scatter(
        head_terms.astype(jnp.bfloat16), "head", scatter_dimension=0, tiled=True
    ).astype(jnp.float32)
    block_resid = (
        lax.dynamic_slice_in_dim(embedded, first_token, head_rows, 0).astype(jnp.float32)
        + block_sum
    )
    block_normed = (block_resid * rms_scale(block_resid) * norm_gain).astype(jnp.bfloat16)
    normed = lax.all_gather(block_normed, "head", axis=0, tiled=True)
    active = jax.nn.gelu(jnp.dot(normed, wide_weight, preferred_element_type=jnp.float32)).astype(
        jnp.bfloat16
    )
    block_mix = lax.psum_scatter(
        lax.dot_general(
            active, narrow_weight, contract_last, preferred_element_type=jnp.float32
        ).astype(jnp.bfloat16),
        "head",
        scatter_dimension=0,
        tiled=True,
    ).astype(jnp.float32)
    block_after = block_resid + block_mix
    after_scale = rms_scale(block_after)
    decoded_in = (block_after * after_scale * decode_gain).astype(jnp.bfloat16)
    logits = jnp.dot(decoded_in, decode_weight, preferred_element_type=jnp.float32)
    loss_scale = 1.0 / (transient.shape[-1] * math.sqrt(target_total))
    render_rows, grad_logits = pixel_loss(logits, pixels_true[0, 0], transient[0, 0], loss_scale)
    grad_decode_local = lax.dot_general(
        decoded_in, grad_logits, contract_rows, preferred_element_type=jnp.float32
    )
    grad_decoded = lax.dot_general(
        grad_logits, decode_weight, contract_last, preferred_element_type=jnp.float32
    )
    gained = grad_decoded * decode_gain
    cubed = after_scale * after_scale * after_scale
    grad_after = (
        after_scale * gained
        - block_after * cubed * jnp.mean(gained * block_after, axis=1, keepdims=True)
    ).astype(jnp.bfloat16)
    grad_narrow_local = lax.dot_general(
        lax.all_gather(grad_after, "head", axis=0, tiled=True),
        active,
        contract_rows,
        preferred_element_type=jnp.float32,
    )
    decode_heads = lax.psum(grad_decode_local.astype(jnp.bfloat16), "head").astype(jnp.float32)
    grad_decode, grad_narrow = (
        lax.psum_scatter(decode_heads, ("tok", "sub"), scatter_dimension=0, tiled=True),
        lax.psum_scatter(grad_narrow_local, ("tok", "sub"), scatter_dimension=0, tiled=True),
    )
    render = render_rows.reshape(1, 1, render_rows.shape[0], render_rows.shape[1])
    return (render, grad_decode, grad_narrow)


CHUNK_PAD = 16
NT = (((1,), (1,)), ((), ()))
TN = (((0,), (0,)), ((), ()))
MESH = pl.DeviceIdType.MESH


def dot(a, b, dims=None):
    if dims is None:
        dims = (((1,), (0,)), ((), ()))
    return lax.dot_general(a, b, dims, preferred_element_type=jnp.float32)


def dot_exact(a, b, dims):
    return lax.dot_general(
        a, b, dims, precision=lax.Precision.HIGHEST, preferred_element_type=jnp.float32
    )


def softplus(x):
    return jnp.maximum(x, 0.0) + jnp.log1p(jnp.exp(-jnp.abs(x)))


def gelu(x):
    return 0.5 * x * (1.0 + jnp.tanh(0.7978845608028654 * (x + 0.044715 * (x * x * x))))


def scene_kernel(
    tok_n,
    rate_scale,
    loss_scale,
    rb_ref,
    views_ref,
    rays_ref,
    turn_ref,
    anchor_ref,
    rw_ref,
    truth_ref,
    tran_ref,
    ngain_ref,
    dgain_ref,
    x_hbm,
    kw_hbm,
    vw_hbm,
    fast_hbm,
    ray_hbm,
    qw_hbm,
    outw_hbm,
    wide_hbm,
    narrow_hbm,
    decw_hbm,
    render_ref,
    gdec_ref,
    gnar_ref,
    x_ref,
    kw_ref,
    vw_ref,
    start_ref,
    ray_ref,
    qw_ref,
    emb_ref,
    q_ref,
    outw_side,
    wide_side,
    narrow_side,
    act_side,
    outw,
    wide,
    narrow,
    decw,
    gacc,
    startf,
    fsb,
    fpr,
    fps,
    frr,
    ag,
    agp,
    hs,
    hr,
    gs,
    gr,
    active,
    gat,
    dlf,
    dsb,
    dpr,
    dps,
    drr,
    dx,
    dxr,
    gsb,
    gpr,
    gps,
    grr,
    send_sem,
    recv_sem,
    local_sem,
):
    t = lax.axis_index("tok")
    h = lax.axis_index("head")
    g = lax.axis_index("groups")
    s = lax.axis_index("sub")
    so = 1 - s
    core = {"sub": so}
    side = {"head": 1 - h}
    twin = {"groups": 1 - g}

    step_rows = 512
    steps = x_hbm.shape[0] // step_rows
    pairs = [(kw_hbm, kw_ref), (fast_hbm, start_ref), (vw_hbm, vw_ref)]
    pairs += [
        (x_hbm.at[pl.ds(i * step_rows, step_rows)], x_ref.at[pl.ds(i * step_rows, step_rows)])
        for i in range(steps)
    ]
    first_loads = len(pairs)
    pairs += [
        (ray_hbm, ray_ref),
        (qw_hbm, qw_ref),
        (outw_hbm, outw),
        (wide_hbm, wide),
        (narrow_hbm, narrow),
        (decw_hbm, decw),
    ]
    loads = [
        pltpu.make_async_copy(src, dst, local_sem.at[i]) for i, (src, dst) in enumerate(pairs)
    ]
    for load in loads[:first_loads]:
        load.start()
    ray_load, qw_load, outw_load, wide_load, narrow_load, decw_load = loads[first_loads:]

    def chip(k):
        return lax.rem(t + k, tok_n)

    def source(k):
        return lax.rem(t + tok_n - k, tok_n)

    count = [0]

    def remote(src, dst, where):
        i = count[0]
        count[0] += 1
        return pltpu.make_async_remote_copy(
            src_ref=src,
            dst_ref=dst,
            send_sem=send_sem.at[i],
            recv_sem=recv_sem.at[i],
            device_id=where,
            device_id_type=MESH,
        )

    others = list(range(1, tok_n))
    every = others + [0]

    barrier = pltpu.get_barrier_semaphore()
    for where in [core, side, twin] + [{"tok": chip(k)} for k in others]:
        pl.semaphore_signal(barrier, inc=1, device_id=where, device_id_type=MESH)

    for load in loads[:first_loads]:
        load.wait()
    for load in loads[first_loads:]:
        load.start()
    pl.semaphore_wait(barrier, 2 + tok_n)

    def quarter(ref, g_, s_):
        n = ref.shape[0] // 4
        return ref.at[pl.ds(pl.multiple_of((2 * g_ + s_) * n, n), n)]

    def fetch(hbm, target):
        mine, twins = quarter(target, g, s), quarter(target, 1 - g, s)
        return (
            remote(quarter(hbm, g, s), mine, side),
            remote(mine, mine, twin),
            remote(mine, mine, core),
            remote(twins, twins, core),
        )

    outw_side_in, outw_twin, outw_core, outw_core2 = fetch(outw_hbm, outw_side)
    wide_side_in, wide_twin, wide_core, wide_core2 = fetch(wide_hbm, wide_side)
    narrow_side_in, narrow_twin, narrow_core, narrow_core2 = fetch(narrow_hbm, narrow_side)
    outw_side_in.start()
    wide_side_in.start()

    width = start_ref.shape[1]
    depth = start_ref.shape[2]
    gacc[...] = jnp.zeros_like(gacc)
    rate_rows_w = jnp.broadcast_to(rw_ref[...].astype(jnp.float32), (128, rw_ref.shape[1])).astype(
        jnp.bfloat16
    )

    def token_step(i, carry):
        x = x_ref[pl.ds(pl.multiple_of(i * step_rows, step_rows), step_rows), :]
        keys_raw = dot(x, kw_ref[...], NT)
        keys = (keys_raw * rms_scale(keys_raw)).astype(jnp.bfloat16)
        values = dot(x, vw_ref[...], NT).astype(jnp.bfloat16)
        logit = dot(x, rate_rows_w, NT)[:, 0:1] + rb_ref[0]
        rate = softplus(logit) * rate_scale
        descent = (-rate * values.astype(jnp.float32)).astype(jnp.bfloat16)
        pre_first = dot(keys, start_ref[0])
        pre_third = dot(keys, start_ref[1])
        sig = jax.nn.sigmoid(pre_first)
        silu = pre_first * sig
        hidden = (silu * pre_third).astype(jnp.bfloat16)
        grad_hidden = dot(descent, start_ref[2])
        grad_first = (grad_hidden * pre_third * (sig * (1.0 + pre_first * (1.0 - sig)))).astype(
            jnp.bfloat16
        )
        grad_third = (grad_hidden * silu).astype(jnp.bfloat16)
        gacc[0:width] += dot(keys, grad_first, TN)
        gacc[width : 2 * width] += dot(keys, grad_third, TN)
        gacc[2 * width : 3 * width] += dot(descent, hidden, TN)
        return carry

    lax.fori_loop(0, steps, token_step, 0)
    for m in range(3):
        startf[m * width : (m + 1) * width] = start_ref[m].astype(jnp.float32)

    rows = 3 * width // (2 * tok_n)
    pad = fsb.shape[1] - rows

    def padded(v):
        return jnp.concatenate([v, jnp.zeros((pad, depth), jnp.float32)], axis=0).astype(
            jnp.bfloat16
        )

    def fast_rows(c, sub):
        return pl.ds(pl.multiple_of((c * 2 + sub) * rows, 8), rows)

    fast_pair = {}
    for k in every:
        fsb[k] = padded(gacc[fast_rows(chip(k), so)])
        fast_pair[k] = remote(fsb.at[k], fpr.at[k], core)
        fast_pair[k].start()
    outw_side_in.wait_recv()
    outw_twin.start()
    outw_core.start()
    narrow_side_in.start()
    fast_chip = {}
    for k in others:
        fast_pair[k].wait_recv()
        fps[k] = padded(gacc[fast_rows(chip(k), s)] + fpr[k][:rows].astype(jnp.float32))
        fast_chip[k] = remote(fps.at[k], frr.at[k], {"tok": chip(k)})
        fast_chip[k].start()

    views = views_ref[...][None, :]
    rays = rays_ref[...][None, :]
    cameras = turn_ref.shape[1]
    targets = views.shape[1]
    chosen = jnp.where(
        lax.broadcasted_iota(jnp.int32, (cameras, targets), 0) == views, 1.0, 0.0
    ).astype(jnp.float32)
    plain = (((1,), (0,)), ((), ()))
    across = IMG // PATCH
    table = jnp.concatenate(
        [
            dot_exact(turn_ref[...], chosen, plain),
            dot_exact(anchor_ref[...], chosen, plain),
            jnp.bitwise_and(rays, across - 1).astype(jnp.float32),
            lax.shift_right_logical(rays, across.bit_length() - 1).astype(jnp.float32),
            jnp.zeros((2, targets), jnp.float32),
        ],
        axis=0,
    ).T

    def entry(i):
        return table[:, i : i + 1]

    spots = lax.broadcasted_iota(jnp.int32, (1, PATCH * PATCH), 1)
    spot_x = jnp.bitwise_and(spots, PATCH - 1).astype(jnp.float32)
    spot_y = lax.shift_right_logical(spots, PATCH.bit_length() - 1).astype(jnp.float32)
    camera_x = (entry(12) * PATCH + spot_x + 0.5 - 0.5 * IMG) / IMG
    camera_y = (entry(13) * PATCH + spot_y + 0.5 - 0.5 * IMG) / IMG
    dir_x = (1.0 + entry(0)) * camera_x + entry(1) * camera_y + entry(2)
    dir_y = entry(3) * camera_x + (1.0 + entry(4)) * camera_y + entry(5)
    dir_z = entry(6) * camera_x + entry(7) * camera_y + (1.0 + entry(8))
    norm_inv = lax.rsqrt(dir_x * dir_x + dir_y * dir_y + dir_z * dir_z)
    dir_x = dir_x * norm_inv
    dir_y = dir_y * norm_inv
    dir_z = dir_z * norm_inv
    features = jnp.concatenate(
        [
            dir_x,
            dir_y,
            dir_z,
            entry(10) * dir_z - entry(11) * dir_y,
            entry(11) * dir_x - entry(9) * dir_z,
            entry(9) * dir_y - entry(10) * dir_x,
        ],
        axis=1,
    ).astype(jnp.bfloat16)
    half = emb_ref.shape[1]
    ray_load.wait()
    qw_load.wait()
    embedded = dot(features, ray_ref[...]).astype(jnp.bfloat16)
    query_raw = dot(embedded, qw_ref[...], NT)
    queries = (query_raw * rms_scale(query_raw)).astype(jnp.bfloat16)
    for i in range(2):
        emb_ref[i] = embedded[i * half : (i + 1) * half]
        q_ref[i] = queries[i * half : (i + 1) * half]

    wide_side_in.wait_recv()
    wide_twin.start()
    wide_core.start()
    outw_twin.wait_recv()
    outw_core2.start()
    fast_pair[0].wait_recv()
    gradient = gacc[fast_rows(t, s)] + fpr[0][:rows].astype(jnp.float32)
    for k in others:
        fast_chip[k].wait_recv()
        gradient = gradient + frr[k][:rows].astype(jnp.float32)
    start = startf[fast_rows(t, s)]
    moved = start - gradient
    restore = jnp.sqrt(jnp.mean(start * start, axis=-1, keepdims=True) + EPSILON)
    ag[0] = padded(moved * rms_scale(moved) * restore)

    gather_chip = {k: remote(ag.at[0], ag.at[k], {"tok": chip(k)}) for k in others}
    gather_core = {k: remote(ag.at[k], agp.at[k], core) for k in every}
    for k in others:
        gather_chip[k].start()
    gather_core[0].start()
    narrow_side_in.wait_recv()
    narrow_twin.start()
    narrow_core.start()
    wide_twin.wait_recv()
    wide_core2.start()
    for k in others:
        gather_chip[k].wait_recv()
        gather_core[k].start()
        startf[fast_rows(source(k), s)] = ag[k][:rows].astype(jnp.float32)
    startf[fast_rows(t, s)] = ag[0][:rows].astype(jnp.float32)
    for k in every:
        gather_core[k].wait_recv()
        startf[fast_rows(source(k), so)] = agp[k][:rows].astype(jnp.float32)
    fast = [startf[m * width : (m + 1) * width].astype(jnp.bfloat16) for m in range(3)]

    def head_out(q):
        first = dot(q, fast[0])
        third = dot(q, fast[1])
        hidden = (first * jax.nn.sigmoid(first) * third).astype(jnp.bfloat16)
        return dot(hidden, fast[2], NT).astype(jnp.bfloat16)

    hs[...] = head_out(q_ref[1 - h])
    head_copy = remote(hs, hr, side)
    head_copy.start()
    own_out = head_out(q_ref[h])
    outw_load.wait()
    outw_core.wait_recv()
    outw_core2.wait_recv()
    resid = emb_ref[h].astype(jnp.float32) + dot(own_out, outw[...])
    head_copy.wait_recv()
    resid = resid + dot(hr[...], outw_side[...])
    normed = (resid * rms_scale(resid) * ngain_ref[...][None, :]).astype(jnp.bfloat16)

    wide_load.wait()
    wide_core.wait_recv()
    wide_core2.wait_recv()
    act_side[...] = gelu(dot(normed, wide_side[...])).astype(jnp.bfloat16)
    act_copy = remote(act_side, active.at[pl.ds(half, half)], side)
    act_copy.start()
    active[0:half] = gelu(dot(normed, wide[...])).astype(jnp.bfloat16)
    narrow_load.wait()
    mixed = dot(active[0:half], narrow[...], NT)
    narrow_twin.wait_recv()
    narrow_core2.start()
    narrow_core.wait_recv()
    narrow_core2.wait_recv()
    after = resid + (mixed + dot(act_side[...], narrow_side[...], NT))
    truth = truth_ref[...].astype(jnp.float32)
    keep = (1 - tran_ref[...]).astype(jnp.float32).T
    pixels = keep.shape[1]
    spot = lax.broadcasted_iota(jnp.int32, (pixels, 3 * pixels), 1) - 3 * (
        lax.broadcasted_iota(jnp.int32, (pixels, 3 * pixels), 0)
    )
    spread_out = jnp.where((spot >= 0) & (spot < 3), 1.0, 0.0).astype(jnp.float32)
    decw_load.wait()
    after_scale = rms_scale(after)
    decoded = (after * after_scale * dgain_ref[...][None, :]).astype(jnp.bfloat16)
    logits = dot(decoded, decw[...])

    colors = logits[:, : 3 * pixels]
    render_ref[...] = colors.astype(jnp.bfloat16)
    spread_logit = logits[:, 3 * pixels :]
    spread = softplus(spread_logit) + BETA_FLOOR
    error = colors - truth
    squared = dot_exact(error * error, spread_out, NT)
    inverse = 1.0 / (spread * spread)
    weight = dot_exact(keep * inverse * loss_scale, spread_out, (((1,), (0,)), ((), ())))
    grad_spread = (
        keep
        * (1.0 / spread - squared * inverse / spread)
        * loss_scale
        * jax.nn.sigmoid(spread_logit)
    )
    grad_logits = jnp.concatenate([weight * error, grad_spread], axis=1).astype(jnp.bfloat16)
    grad_decoded = dot(grad_logits, decw[...], NT)
    gained = grad_decoded * dgain_ref[...][None, :]
    cubed = after_scale * after_scale * after_scale
    gs[...] = (
        after_scale * gained
        - after * cubed * jnp.mean(gained * after, axis=1, keepdims=True)
    ).astype(jnp.bfloat16)
    grad_copy = remote(gs, gr, side)
    grad_copy.start()

    part = gdec_ref.shape[0]

    def part_rows(c, sub):
        return pl.ds(pl.multiple_of((c * 2 + sub) * part, 8), part)

    dlf[...] = dot(decoded, grad_logits, TN)
    dec_pair = {}
    for k in every:
        dsb[k] = dlf[part_rows(chip(k), so)].astype(jnp.bfloat16)
        dec_pair[k] = remote(dsb.at[k], dpr.at[k], core)
        dec_pair[k].start()

    dec_chip = {}
    for k in others:
        dec_pair[k].wait_recv()
        dps[k] = (dlf[part_rows(chip(k), s)] + dpr[k].astype(jnp.float32)).astype(jnp.bfloat16)
        dec_chip[k] = remote(dps.at[k], drr.at[k], {"tok": chip(k)})
        dec_chip[k].start()

    grad_copy.wait_recv()
    act_copy.wait_recv()
    both = jnp.concatenate([gs[...].astype(jnp.float32), gr[...].astype(jnp.float32)], axis=0)
    both_t = both.T
    for i in range(2 * tok_n):
        gat[i] = both_t[i * part : (i + 1) * part].astype(jnp.bfloat16)
    nar_pair = {}
    for k in every:
        gsb[k] = dot(gat[chip(k) * 2 + so], active[...]).astype(jnp.bfloat16)
        nar_pair[k] = remote(gsb.at[k], gpr.at[k], core)
        nar_pair[k].start()
    nar_chip = {}
    for k in others:
        mine = dot(gat[chip(k) * 2 + s], active[...])
        nar_pair[k].wait_recv()
        gps[k] = (mine + gpr[k].astype(jnp.float32)).astype(jnp.bfloat16)
        nar_chip[k] = remote(gps.at[k], grr.at[k], {"tok": chip(k)})
        nar_chip[k].start()
    dec_pair[0].wait_recv()
    dec_sum = dlf[part_rows(t, s)] + dpr[0].astype(jnp.float32)
    for k in others:
        dec_chip[k].wait_recv()
        dec_sum = dec_sum + drr[k].astype(jnp.float32)
    dx[...] = dec_sum
    dec_side = remote(dx, dxr, side)
    dec_side.start()
    nar_pair[0].wait_recv()
    gnar_ref[...] = dot(gat[t * 2 + s], active[...]) + gpr[0].astype(jnp.float32)
    dec_side.wait_recv()
    gdec_ref[...] = dec_sum + dxr[...]
    for k in others:
        nar_chip[k].wait_recv()
        gnar_ref[...] += grr[k].astype(jnp.float32)

    for group in (
        fast_pair,
        fast_chip,
        gather_chip,
        gather_core,
        dec_pair,
        nar_pair,
        dec_chip,
        nar_chip,
    ):
        for copy in group.values():
            copy.wait_send()
    for copy in (
        head_copy,
        act_copy,
        grad_copy,
        dec_side,
        outw_side_in,
        outw_twin,
        outw_core,
        outw_core2,
        wide_side_in,
        wide_twin,
        wide_core,
        wide_core2,
        narrow_side_in,
        narrow_twin,
        narrow_core,
        narrow_core2,
    ):
        copy.wait_send()


def hand_out(*refs):
    count = len(refs) // 2
    copies = [
        pltpu.make_async_copy(refs[i], refs[count + i], refs[-1].at[i]) for i in range(count)
    ]
    for copy in copies:
        copy.start()
    for copy in copies:
        copy.wait()


def on_device_kernel(
    in_tokens,
    target_views,
    target_rays,
    camera_turn,
    camera_anchor,
    pixels_true,
    transient,
    query_weight,
    key_weight,
    value_weight,
    rate_weight,
    rate_bias,
    fast_init,
    out_weight,
    ray_weight,
    norm_gain,
    wide_weight,
    narrow_weight,
    decode_gain,
    decode_weight,
):
    tok_n = lax.axis_size("tok")
    devices = tok_n * lax.axis_size("sub")
    in_total = in_tokens.shape[0] * devices
    target_total = target_views.shape[0] * devices
    half = pixels_true.shape[2]
    model = in_tokens.shape[1]
    hidden = wide_weight.shape[1]
    width, depth = fast_init.shape[2:]
    fast_rows = -(-(3 * width // devices) // CHUNK_PAD) * CHUNK_PAD
    part = model // devices
    logit_n = decode_weight.shape[1]
    vmem = pl.BlockSpec(memory_space=pltpu.VMEM)
    anywhere = pl.BlockSpec(memory_space=pl.ANY)
    bf16, f32 = jnp.bfloat16, jnp.float32
    fast_buf = pltpu.VMEM((tok_n, fast_rows, depth), bf16)
    row_buf = pltpu.VMEM((half, model), bf16)
    dec_buf = pltpu.VMEM((tok_n, part, logit_n), bf16)
    nar_buf = pltpu.VMEM((tok_n, part, hidden), bf16)
    copies = 4 * tok_n + 4 * (tok_n - 1) + 16
    render, grad_decode, grad_narrow = pl.pallas_call(
        functools.partial(
            scene_kernel,
            tok_n,
            RATE_SCALE / math.sqrt(in_total),
            1.0 / (transient.shape[-1] * math.sqrt(target_total)),
        ),
        out_shape=(
            jax.ShapeDtypeStruct((half, pixels_true.shape[3]), bf16),
            jax.ShapeDtypeStruct((part, logit_n), f32),
            jax.ShapeDtypeStruct((part, hidden), f32),
        ),
        in_specs=[pl.BlockSpec(memory_space=pltpu.SMEM)] + [vmem] * 9 + [anywhere] * 10,
        out_specs=(vmem, vmem, vmem),
        scratch_shapes=[
            pltpu.VMEM(in_tokens.shape, bf16),
            pltpu.VMEM((width, model), bf16),
            pltpu.VMEM((width, model), bf16),
            pltpu.VMEM((3, width, depth), bf16),
            pltpu.VMEM(ray_weight.shape, bf16),
            pltpu.VMEM((width, model), bf16),
            pltpu.VMEM((2, half, model), bf16),
            pltpu.VMEM((2, half, width), bf16),
            pltpu.VMEM(out_weight.shape, bf16),
            pltpu.VMEM(wide_weight.shape, bf16),
            pltpu.VMEM(narrow_weight.shape, bf16),
            pltpu.VMEM((half, hidden), bf16),
            pltpu.VMEM(out_weight.shape, bf16),
            pltpu.VMEM(wide_weight.shape, bf16),
            pltpu.VMEM(narrow_weight.shape, bf16),
            pltpu.VMEM(decode_weight.shape, bf16),
            pltpu.VMEM((3 * width, depth), f32),
            pltpu.VMEM((3 * width, depth), f32),
        ]
        + [fast_buf] * 6
        + [pltpu.VMEM((half, width), bf16)] * 2
        + [row_buf] * 2
        + [
            pltpu.VMEM((2 * half, hidden), bf16),
            pltpu.VMEM((devices, part, 2 * half), bf16),
            pltpu.VMEM((model, logit_n), f32),
        ]
        + [dec_buf] * 4
        + [pltpu.VMEM((part, logit_n), f32)] * 2
        + [nar_buf] * 4
        + [
            pltpu.SemaphoreType.DMA((copies,)),
            pltpu.SemaphoreType.DMA((copies,)),
            pltpu.SemaphoreType.DMA((9 + in_tokens.shape[0] // 512,)),
        ],
        compiler_params=pltpu.CompilerParams(
            collective_id=0, has_side_effects=True, vmem_limit_bytes=60 * 2**20
        ),
    )(
        rate_bias,
        target_views,
        target_rays,
        camera_turn.T,
        camera_anchor.T,
        rate_weight.T,
        pixels_true[0, 0],
        transient[0, 0].T,
        norm_gain,
        decode_gain,
        in_tokens,
        key_weight.T,
        value_weight.T,
        fast_init[0],
        ray_weight,
        query_weight.T,
        out_weight,
        wide_weight,
        narrow_weight,
        decode_weight,
    )
    render, grad_decode, grad_narrow = pl.pallas_call(
        hand_out,
        out_shape=tuple(
            jax.ShapeDtypeStruct(v.shape, v.dtype) for v in (render, grad_decode, grad_narrow)
        ),
        in_specs=[anywhere] * 3,
        out_specs=(anywhere,) * 3,
        scratch_shapes=[pltpu.SemaphoreType.DMA((3,))],
    )(render, grad_decode, grad_narrow)
    return (render[None, None], grad_decode, grad_narrow)


def kernel_fits(mesh):
    return mesh.shape["groups"] == 2 and mesh.shape["head"] == 2 and (
        mesh.shape["sub"] == 2 and mesh.shape["tok"] in (2, 4)
    )


def solution(mesh):
    in_specs = (
        P(("groups", "tok", "sub"), None),
        P(("groups", "tok", "sub")),
        P(("groups", "tok", "sub")),
        P("groups", None),
        P("groups", None),
        P(("groups", "tok", "sub"), "head", None, None),
        P(("groups", "tok", "sub"), "head", None, None),
        P(None, "head"),
        P(None, "head"),
        P(None, "head"),
        P(None, "head"),
        P("head"),
        P("head", None, None, None),
        P("head", None),
        P(),
        P(),
        P(None, "head"),
        P(None, "head"),
        P(),
        P(),
    )
    out_specs = (
        P(("groups", "tok", "sub"), "head", None, None),
        P(("groups", "tok", "sub"), None),
        P(("groups", "tok", "sub"), "head"),
    )
    body = on_device_kernel if kernel_fits(mesh) else on_device
    return jax.shard_map(
        body, mesh=mesh, in_specs=in_specs, out_specs=out_specs, check_vma=False
    )
```

```python
import functools
import math

import jax
import jax.numpy as jnp
from jax import lax
from jax.experimental import pallas as pl
from jax.experimental.pallas import tpu as pltpu
from jax.sharding import PartitionSpec as P

PATCH = 8
IMG = 256


EPSILON = 1e-06
RATE_SCALE = 0.2
BETA_FLOOR = 0.05


def rms_scale(vector):
    return lax.rsqrt(jnp.mean(vector * vector, axis=-1, keepdims=True) + EPSILON)


def silu_grad(activation_in):
    sigmoid_part = jax.nn.sigmoid(activation_in)
    return sigmoid_part * (1.0 + activation_in * (1.0 - sigmoid_part))


def plucker_rays(view_ids, ray_ids, camera_turn, camera_anchor):
    camera_count = camera_turn.shape[0]
    one_hot = view_ids[:, None] == jnp.arange(camera_count, dtype=jnp.int32)[None, :]
    turn_rows = jnp.sum(jnp.where(one_hot[:, :, None], camera_turn[None, :, :], 0.0), axis=1)
    anchor_rows = jnp.sum(jnp.where(one_hot[:, :, None], camera_anchor[None, :, :], 0.0), axis=1)
    patch_across = IMG // PATCH
    patch_row = ray_ids // patch_across
    patch_col = ray_ids % patch_across
    pixel_index = jnp.arange(PATCH * PATCH, dtype=jnp.int32)
    column_pos = (patch_col[:, None] * PATCH + pixel_index[None, :] % PATCH).astype(
        jnp.float32
    ) + 0.5
    row_pos = (patch_row[:, None] * PATCH + pixel_index[None, :] // PATCH).astype(jnp.float32) + 0.5
    camera_x = (column_pos - 0.5 * IMG) / IMG
    camera_y = (row_pos - 0.5 * IMG) / IMG
    dir_x = (1.0 + turn_rows[:, 0:1]) * camera_x + turn_rows[:, 1:2] * camera_y + turn_rows[:, 2:3]
    dir_y = turn_rows[:, 3:4] * camera_x + (1.0 + turn_rows[:, 4:5]) * camera_y + turn_rows[:, 5:6]
    dir_z = turn_rows[:, 6:7] * camera_x + turn_rows[:, 7:8] * camera_y + (1.0 + turn_rows[:, 8:9])
    norm_inv = lax.rsqrt(dir_x * dir_x + dir_y * dir_y + dir_z * dir_z)
    dir_x = dir_x * norm_inv
    dir_y = dir_y * norm_inv
    dir_z = dir_z * norm_inv
    anchor_x = anchor_rows[:, 0:1]
    anchor_y = anchor_rows[:, 1:2]
    anchor_z = anchor_rows[:, 2:3]
    moment_x = anchor_y * dir_z - anchor_z * dir_y
    moment_y = anchor_z * dir_x - anchor_x * dir_z
    moment_z = anchor_x * dir_y - anchor_y * dir_x
    return jnp.concatenate([dir_x, dir_y, dir_z, moment_x, moment_y, moment_z], axis=1).astype(
        jnp.bfloat16
    )


def fast_gradient(keys_normed, value_rows, rate_rows, weights):
    pre_first = jnp.dot(keys_normed, weights[0], preferred_element_type=jnp.float32)
    pre_third = jnp.dot(keys_normed, weights[1], preferred_element_type=jnp.float32)
    fast_hidden = (jax.nn.silu(pre_first) * pre_third).astype(jnp.bfloat16)
    descent = (-rate_rows[:, None] * value_rows.astype(jnp.float32)).astype(jnp.bfloat16)
    contract_rows = (((0,), (0,)), ((), ()))
    grad_second = lax.dot_general(
        descent, fast_hidden, contract_rows, preferred_element_type=jnp.float32
    )
    grad_hidden = jnp.dot(descent, weights[2], preferred_element_type=jnp.float32)
    grad_pre_first = (grad_hidden * pre_third * silu_grad(pre_first)).astype(jnp.bfloat16)
    grad_pre_third = (grad_hidden * jax.nn.silu(pre_first)).astype(jnp.bfloat16)
    grad_first = lax.dot_general(
        keys_normed, grad_pre_first, contract_rows, preferred_element_type=jnp.float32
    )
    grad_third = lax.dot_general(
        keys_normed, grad_pre_third, contract_rows, preferred_element_type=jnp.float32
    )
    return jnp.stack([grad_first, grad_third, grad_second])


def renormalize(gradient, start_rows):
    start_float = start_rows.astype(jnp.float32)
    moved_rows = start_float - gradient
    restore = jnp.sqrt(jnp.mean(start_float * start_float, axis=-1, keepdims=True) + EPSILON)
    return (moved_rows * rms_scale(moved_rows) * restore).astype(jnp.bfloat16)


def apply_fast(query_rows, weights):
    apply_first = jnp.dot(query_rows, weights[0], preferred_element_type=jnp.float32)
    apply_third = jnp.dot(query_rows, weights[1], preferred_element_type=jnp.float32)
    apply_hidden = (jax.nn.silu(apply_first) * apply_third).astype(jnp.bfloat16)
    contract_last = (((1,), (1,)), ((), ()))
    return lax.dot_general(
        apply_hidden, weights[2], contract_last, preferred_element_type=jnp.float32
    ).astype(jnp.bfloat16)


def pixel_loss(logits, truth_rows, transient_bits, loss_scale):
    pixel_count = transient_bits.shape[-1]
    row_total = logits.shape[0]
    colors = logits[:, : 3 * pixel_count]
    spread_logit = logits[:, 3 * pixel_count :]
    spread = jax.nn.softplus(spread_logit) + BETA_FLOOR
    error_rows = colors.reshape(row_total, pixel_count, 3) - truth_rows.reshape(
        row_total, pixel_count, 3
    ).astype(jnp.float32)
    squared = jnp.sum(error_rows * error_rows, axis=2)
    keep_mask = (1 - transient_bits).astype(jnp.float32)
    inverse = 1.0 / (spread * spread)
    grad_colors = (keep_mask * inverse * loss_scale)[:, :, None] * error_rows
    grad_spread = (
        keep_mask
        * (1.0 / spread - squared * inverse / spread)
        * loss_scale
        * jax.nn.sigmoid(spread_logit)
    )
    grad_logits = jnp.concatenate(
        [grad_colors.reshape(row_total, 3 * pixel_count), grad_spread], axis=1
    ).astype(jnp.bfloat16)
    return (colors.astype(jnp.bfloat16), grad_logits)


def on_device(
    in_tokens,
    target_views,
    target_rays,
    camera_turn,
    camera_anchor,
    pixels_true,
    transient,
    query_weight,
    key_weight,
    value_weight,
    rate_weight,
    rate_bias,
    fast_init,
    out_weight,
    ray_weight,
    norm_gain,
    wide_weight,
    narrow_weight,
    decode_gain,
    decode_weight,
):
    token_devices = lax.axis_size("tok") * lax.axis_size("sub")
    in_total = in_tokens.shape[0] * token_devices
    target_total = target_views.shape[0] * token_devices
    contract_last = (((1,), (1,)), ((), ()))
    contract_rows = (((0,), (0,)), ((), ()))
    keys_raw = jnp.dot(in_tokens, key_weight, preferred_element_type=jnp.float32)
    keys_normed = (keys_raw * rms_scale(keys_raw)).astype(jnp.bfloat16)
    value_rows = jnp.dot(in_tokens, value_weight, preferred_element_type=jnp.float32).astype(
        jnp.bfloat16
    )
    rate_logit = jnp.dot(in_tokens, rate_weight, preferred_element_type=jnp.float32) + rate_bias
    rate_rows = jax.nn.softplus(rate_logit[:, 0]) * (RATE_SCALE / math.sqrt(in_total))
    start_weights = fast_init[0]
    local_grads = fast_gradient(keys_normed, value_rows, rate_rows, start_weights)
    owned_share = lax.psum_scatter(local_grads, ("tok", "sub"), scatter_dimension=1, tiled=True)
    row_count = owned_share.shape[1]
    first_row = lax.axis_index(("tok", "sub")) * row_count
    fresh_rows = renormalize(
        owned_share, lax.dynamic_slice_in_dim(start_weights, first_row, row_count, 1)
    )
    new_weights = lax.all_gather(fresh_rows, ("tok", "sub"), axis=1, tiled=True)
    features = plucker_rays(target_views, target_rays, camera_turn, camera_anchor)
    embedded = jnp.dot(features, ray_weight, preferred_element_type=jnp.float32).astype(
        jnp.bfloat16
    )
    query_raw = jnp.dot(embedded, query_weight, preferred_element_type=jnp.float32)
    queries = (query_raw * rms_scale(query_raw)).astype(jnp.bfloat16)
    applied = apply_fast(queries, new_weights)
    head_terms = jnp.dot(applied, out_weight, preferred_element_type=jnp.float32)
    head_rows = pixels_true.shape[2]
    first_token = lax.axis_index("head") * head_rows
    block_sum = lax.psum_scatter(
        head_terms.astype(jnp.bfloat16), "head", scatter_dimension=0, tiled=True
    ).astype(jnp.float32)
    block_resid = (
        lax.dynamic_slice_in_dim(embedded, first_token, head_rows, 0).astype(jnp.float32)
        + block_sum
    )
    block_normed = (block_resid * rms_scale(block_resid) * norm_gain).astype(jnp.bfloat16)
    normed = lax.all_gather(block_normed, "head", axis=0, tiled=True)
    active = jax.nn.gelu(jnp.dot(normed, wide_weight, preferred_element_type=jnp.float32)).astype(
        jnp.bfloat16
    )
    block_mix = lax.psum_scatter(
        lax.dot_general(
            active, narrow_weight, contract_last, preferred_element_type=jnp.float32
        ).astype(jnp.bfloat16),
        "head",
        scatter_dimension=0,
        tiled=True,
    ).astype(jnp.float32)
    block_after = block_resid + block_mix
    after_scale = rms_scale(block_after)
    decoded_in = (block_after * after_scale * decode_gain).astype(jnp.bfloat16)
    logits = jnp.dot(decoded_in, decode_weight, preferred_element_type=jnp.float32)
    loss_scale = 1.0 / (transient.shape[-1] * math.sqrt(target_total))
    render_rows, grad_logits = pixel_loss(logits, pixels_true[0, 0], transient[0, 0], loss_scale)
    grad_decode_local = lax.dot_general(
        decoded_in, grad_logits, contract_rows, preferred_element_type=jnp.float32
    )
    grad_decoded = lax.dot_general(
        grad_logits, decode_weight, contract_last, preferred_element_type=jnp.float32
    )
    gained = grad_decoded * decode_gain
    cubed = after_scale * after_scale * after_scale
    grad_after = (
        after_scale * gained
        - block_after * cubed * jnp.mean(gained * block_after, axis=1, keepdims=True)
    ).astype(jnp.bfloat16)
    grad_narrow_local = lax.dot_general(
        lax.all_gather(grad_after, "head", axis=0, tiled=True),
        active,
        contract_rows,
        preferred_element_type=jnp.float32,
    )
    decode_heads = lax.psum(grad_decode_local.astype(jnp.bfloat16), "head").astype(jnp.float32)
    grad_decode, grad_narrow = (
        lax.psum_scatter(decode_heads, ("tok", "sub"), scatter_dimension=0, tiled=True),
        lax.psum_scatter(grad_narrow_local, ("tok", "sub"), scatter_dimension=0, tiled=True),
    )
    render = render_rows.reshape(1, 1, render_rows.shape[0], render_rows.shape[1])
    return (render, grad_decode, grad_narrow)


CHUNK_PAD = 16
NT = (((1,), (1,)), ((), ()))
TN = (((0,), (0,)), ((), ()))
MESH = pl.DeviceIdType.MESH


def dot(a, b, dims=None):
    if dims is None:
        dims = (((1,), (0,)), ((), ()))
    return lax.dot_general(a, b, dims, preferred_element_type=jnp.float32)


def dot_exact(a, b, dims):
    return lax.dot_general(
        a, b, dims, precision=lax.Precision.HIGHEST, preferred_element_type=jnp.float32
    )


def softplus(x):
    return jnp.maximum(x, 0.0) + jnp.log1p(jnp.exp(-jnp.abs(x)))


def gelu(x):
    return 0.5 * x * (1.0 + jnp.tanh(0.7978845608028654 * (x + 0.044715 * (x * x * x))))


def scene_kernel(
    tok_n,
    rate_scale,
    loss_scale,
    rb_ref,
    views_ref,
    rays_ref,
    turn_ref,
    anchor_ref,
    rw_ref,
    truth_ref,
    tran_ref,
    ngain_ref,
    dgain_ref,
    x_hbm,
    kw_hbm,
    vw_hbm,
    fast_hbm,
    ray_hbm,
    qw_hbm,
    outw_hbm,
    wide_hbm,
    narrow_hbm,
    decw_hbm,
    render_ref,
    gdec_ref,
    gnar_ref,
    x_ref,
    kw_ref,
    vw_ref,
    start_ref,
    ray_ref,
    qw_ref,
    emb_ref,
    q_ref,
    outw_side,
    wide_side,
    narrow_side,
    act_side,
    outw,
    wide,
    narrow,
    decw,
    gacc,
    startf,
    fsb,
    fpr,
    fps,
    frr,
    ag,
    agp,
    hs,
    hr,
    gs,
    gr,
    active,
    gat,
    dlf,
    dsb,
    dpr,
    dps,
    drr,
    dx,
    dxr,
    gsb,
    gpr,
    gps,
    grr,
    send_sem,
    recv_sem,
    local_sem,
):
    t = lax.axis_index("tok")
    h = lax.axis_index("head")
    g = lax.axis_index("groups")
    s = lax.axis_index("sub")
    so = 1 - s
    core = {"sub": so}
    side = {"head": 1 - h}
    twin = {"groups": 1 - g}

    step_rows = 512
    steps = x_hbm.shape[0] // step_rows
    pairs = [(kw_hbm, kw_ref), (fast_hbm, start_ref), (vw_hbm, vw_ref)]
    pairs += [
        (x_hbm.at[pl.ds(i * step_rows, step_rows)], x_ref.at[pl.ds(i * step_rows, step_rows)])
        for i in range(steps)
    ]
    first_loads = len(pairs)
    pairs += [
        (ray_hbm, ray_ref),
        (qw_hbm, qw_ref),
        (outw_hbm, outw),
        (wide_hbm, wide),
        (narrow_hbm, narrow),
        (decw_hbm, decw),
    ]
    loads = [
        pltpu.make_async_copy(src, dst, local_sem.at[i]) for i, (src, dst) in enumerate(pairs)
    ]
    for load in loads[:first_loads]:
        load.start()
    ray_load, qw_load, outw_load, wide_load, narrow_load, decw_load = loads[first_loads:]

    def chip(k):
        return lax.rem(t + k, tok_n)

    def source(k):
        return lax.rem(t + tok_n - k, tok_n)

    count = [0]

    def remote(src, dst, where):
        i = count[0]
        count[0] += 1
        return pltpu.make_async_remote_copy(
            src_ref=src,
            dst_ref=dst,
            send_sem=send_sem.at[i],
            recv_sem=recv_sem.at[i],
            device_id=where,
            device_id_type=MESH,
        )

    others = list(range(1, tok_n))
    every = others + [0]

    barrier = pltpu.get_barrier_semaphore()
    for where in [core, side, twin] + [{"tok": chip(k)} for k in others]:
        pl.semaphore_signal(barrier, inc=1, device_id=where, device_id_type=MESH)

    for load in loads[:first_loads]:
        load.wait()
    for load in loads[first_loads:]:
        load.start()
    pl.semaphore_wait(barrier, 2 + tok_n)

    def quarter(ref, g_, s_):
        n = ref.shape[0] // 4
        return ref.at[pl.ds(pl.multiple_of((2 * g_ + s_) * n, n), n)]

    def fetch(hbm, target):
        mine, twins = quarter(target, g, s), quarter(target, 1 - g, s)
        return (
            remote(quarter(hbm, g, s), mine, side),
            remote(mine, mine, twin),
            remote(mine, mine, core),
            remote(twins, twins, core),
        )

    outw_side_in, outw_twin, outw_core, outw_core2 = fetch(outw_hbm, outw_side)
    wide_side_in, wide_twin, wide_core, wide_core2 = fetch(wide_hbm, wide_side)
    narrow_side_in, narrow_twin, narrow_core, narrow_core2 = fetch(narrow_hbm, narrow_side)
    outw_side_in.start()
    wide_side_in.start()

    width = start_ref.shape[1]
    depth = start_ref.shape[2]
    gacc[...] = jnp.zeros_like(gacc)
    rate_rows_w = jnp.broadcast_to(rw_ref[...].astype(jnp.float32), (128, rw_ref.shape[1])).astype(
        jnp.bfloat16
    )

    def token_step(i, carry):
        x = x_ref[pl.ds(pl.multiple_of(i * step_rows, step_rows), step_rows), :]
        keys_raw = dot(x, kw_ref[...], NT)
        keys = (keys_raw * rms_scale(keys_raw)).astype(jnp.bfloat16)
        values = dot(x, vw_ref[...], NT).astype(jnp.bfloat16)
        logit = dot(x, rate_rows_w, NT)[:, 0:1] + rb_ref[0]
        rate = softplus(logit) * rate_scale
        descent = (-rate * values.astype(jnp.float32)).astype(jnp.bfloat16)
        pre_first = dot(keys, start_ref[0])
        pre_third = dot(keys, start_ref[1])
        sig = jax.nn.sigmoid(pre_first)
        silu = pre_first * sig
        hidden = (silu * pre_third).astype(jnp.bfloat16)
        grad_hidden = dot(descent, start_ref[2])
        grad_first = (grad_hidden * pre_third * (sig * (1.0 + pre_first * (1.0 - sig)))).astype(
            jnp.bfloat16
        )
        grad_third = (grad_hidden * silu).astype(jnp.bfloat16)
        gacc[0:width] += dot(keys, grad_first, TN)
        gacc[width : 2 * width] += dot(keys, grad_third, TN)
        gacc[2 * width : 3 * width] += dot(descent, hidden, TN)
        return carry

    lax.fori_loop(0, steps, token_step, 0)
    for m in range(3):
        startf[m * width : (m + 1) * width] = start_ref[m].astype(jnp.float32)

    rows = 3 * width // (2 * tok_n)
    pad = fsb.shape[1] - rows

    def padded(v):
        return jnp.concatenate([v, jnp.zeros((pad, depth), jnp.float32)], axis=0).astype(
            jnp.bfloat16
        )

    def fast_rows(c, sub):
        return pl.ds(pl.multiple_of((c * 2 + sub) * rows, 8), rows)

    fast_pair = {}
    for k in every:
        fsb[k] = padded(gacc[fast_rows(chip(k), so)])
        fast_pair[k] = remote(fsb.at[k], fpr.at[k], core)
        fast_pair[k].start()
    outw_side_in.wait_recv()
    outw_twin.start()
    outw_core.start()
    narrow_side_in.start()
    fast_chip = {}
    for k in others:
        fast_pair[k].wait_recv()
        fps[k] = padded(gacc[fast_rows(chip(k), s)] + fpr[k][:rows].astype(jnp.float32))
        fast_chip[k] = remote(fps.at[k], frr.at[k], {"tok": chip(k)})
        fast_chip[k].start()

    views = views_ref[...][None, :]
    rays = rays_ref[...][None, :]
    cameras = turn_ref.shape[1]
    targets = views.shape[1]
    chosen = jnp.where(
        lax.broadcasted_iota(jnp.int32, (cameras, targets), 0) == views, 1.0, 0.0
    ).astype(jnp.float32)
    plain = (((1,), (0,)), ((), ()))
    across = IMG // PATCH
    table = jnp.concatenate(
        [
            dot_exact(turn_ref[...], chosen, plain),
            dot_exact(anchor_ref[...], chosen, plain),
            jnp.bitwise_and(rays, across - 1).astype(jnp.float32),
            lax.shift_right_logical(rays, across.bit_length() - 1).astype(jnp.float32),
            jnp.zeros((2, targets), jnp.float32),
        ],
        axis=0,
    ).T

    def entry(i):
        return table[:, i : i + 1]

    spots = lax.broadcasted_iota(jnp.int32, (1, PATCH * PATCH), 1)
    spot_x = jnp.bitwise_and(spots, PATCH - 1).astype(jnp.float32)
    spot_y = lax.shift_right_logical(spots, PATCH.bit_length() - 1).astype(jnp.float32)
    camera_x = (entry(12) * PATCH + spot_x + 0.5 - 0.5 * IMG) / IMG
    camera_y = (entry(13) * PATCH + spot_y + 0.5 - 0.5 * IMG) / IMG
    dir_x = (1.0 + entry(0)) * camera_x + entry(1) * camera_y + entry(2)
    dir_y = entry(3) * camera_x + (1.0 + entry(4)) * camera_y + entry(5)
    dir_z = entry(6) * camera_x + entry(7) * camera_y + (1.0 + entry(8))
    norm_inv = lax.rsqrt(dir_x * dir_x + dir_y * dir_y + dir_z * dir_z)
    dir_x = dir_x * norm_inv
    dir_y = dir_y * norm_inv
    dir_z = dir_z * norm_inv
    features = jnp.concatenate(
        [
            dir_x,
            dir_y,
            dir_z,
            entry(10) * dir_z - entry(11) * dir_y,
            entry(11) * dir_x - entry(9) * dir_z,
            entry(9) * dir_y - entry(10) * dir_x,
        ],
        axis=1,
    ).astype(jnp.bfloat16)
    half = emb_ref.shape[1]
    ray_load.wait()
    qw_load.wait()
    embedded = dot(features, ray_ref[...]).astype(jnp.bfloat16)
    query_raw = dot(embedded, qw_ref[...], NT)
    queries = (query_raw * rms_scale(query_raw)).astype(jnp.bfloat16)
    for i in range(2):
        emb_ref[i] = embedded[i * half : (i + 1) * half]
        q_ref[i] = queries[i * half : (i + 1) * half]

    wide_side_in.wait_recv()
    wide_twin.start()
    wide_core.start()
    outw_twin.wait_recv()
    outw_core2.start()
    fast_pair[0].wait_recv()
    gradient = gacc[fast_rows(t, s)] + fpr[0][:rows].astype(jnp.float32)
    for k in others:
        fast_chip[k].wait_recv()
        gradient = gradient + frr[k][:rows].astype(jnp.float32)
    start = startf[fast_rows(t, s)]
    moved = start - gradient
    restore = jnp.sqrt(jnp.mean(start * start, axis=-1, keepdims=True) + EPSILON)
    ag[0] = padded(moved * rms_scale(moved) * restore)

    gather_chip = {k: remote(ag.at[0], ag.at[k], {"tok": chip(k)}) for k in others}
    gather_core = {k: remote(ag.at[k], agp.at[k], core) for k in every}
    for k in others:
        gather_chip[k].start()
    gather_core[0].start()
    narrow_side_in.wait_recv()
    narrow_twin.start()
    narrow_core.start()
    wide_twin.wait_recv()
    wide_core2.start()
    for k in others:
        gather_chip[k].wait_recv()
        gather_core[k].start()
        startf[fast_rows(source(k), s)] = ag[k][:rows].astype(jnp.float32)
    startf[fast_rows(t, s)] = ag[0][:rows].astype(jnp.float32)
    for k in every:
        gather_core[k].wait_recv()
        startf[fast_rows(source(k), so)] = agp[k][:rows].astype(jnp.float32)
    fast = [startf[m * width : (m + 1) * width].astype(jnp.bfloat16) for m in range(3)]

    def head_out(q):
        first = dot(q, fast[0])
        third = dot(q, fast[1])
        hidden = (first * jax.nn.sigmoid(first) * third).astype(jnp.bfloat16)
        return dot(hidden, fast[2], NT).astype(jnp.bfloat16)

    hs[...] = head_out(q_ref[1 - h])
    head_copy = remote(hs, hr, side)
    head_copy.start()
    own_out = head_out(q_ref[h])
    outw_load.wait()
    outw_core.wait_recv()
    outw_core2.wait_recv()
    resid = emb_ref[h].astype(jnp.float32) + dot(own_out, outw[...])
    head_copy.wait_recv()
    resid = resid + dot(hr[...], outw_side[...])
    normed = (resid * rms_scale(resid) * ngain_ref[...][None, :]).astype(jnp.bfloat16)

    wide_load.wait()
    wide_core.wait_recv()
    wide_core2.wait_recv()
    act_side[...] = gelu(dot(normed, wide_side[...])).astype(jnp.bfloat16)
    act_copy = remote(act_side, active.at[pl.ds(half, half)], side)
    act_copy.start()
    active[0:half] = gelu(dot(normed, wide[...])).astype(jnp.bfloat16)
    narrow_load.wait()
    mixed = dot(active[0:half], narrow[...], NT)
    narrow_twin.wait_recv()
    narrow_core2.start()
    narrow_core.wait_recv()
    narrow_core2.wait_recv()
    after = resid + (mixed + dot(act_side[...], narrow_side[...], NT))
    truth = truth_ref[...].astype(jnp.float32)
    keep = (1 - tran_ref[...]).astype(jnp.float32).T
    pixels = keep.shape[1]
    spot = lax.broadcasted_iota(jnp.int32, (pixels, 3 * pixels), 1) - 3 * (
        lax.broadcasted_iota(jnp.int32, (pixels, 3 * pixels), 0)
    )
    spread_out = jnp.where((spot >= 0) & (spot < 3), 1.0, 0.0).astype(jnp.float32)
    decw_load.wait()
    after_scale = rms_scale(after)
    decoded = (after * after_scale * dgain_ref[...][None, :]).astype(jnp.bfloat16)
    logits = dot(decoded, decw[...])

    colors = logits[:, : 3 * pixels]
    render_ref[...] = colors.astype(jnp.bfloat16)
    spread_logit = logits[:, 3 * pixels :]
    spread = softplus(spread_logit) + BETA_FLOOR
    error = colors - truth
    squared = dot_exact(error * error, spread_out, NT)
    inverse = 1.0 / (spread * spread)
    weight = dot_exact(keep * inverse * loss_scale, spread_out, (((1,), (0,)), ((), ())))
    grad_spread = (
        keep
        * (1.0 / spread - squared * inverse / spread)
        * loss_scale
        * jax.nn.sigmoid(spread_logit)
    )
    grad_logits = jnp.concatenate([weight * error, grad_spread], axis=1).astype(jnp.bfloat16)
    grad_decoded = dot(grad_logits, decw[...], NT)
    gained = grad_decoded * dgain_ref[...][None, :]
    cubed = after_scale * after_scale * after_scale
    gs[...] = (
        after_scale * gained
        - after * cubed * jnp.mean(gained * after, axis=1, keepdims=True)
    ).astype(jnp.bfloat16)
    grad_copy = remote(gs, gr, side)
    grad_copy.start()

    part = gdec_ref.shape[0]

    def part_rows(c, sub):
        return pl.ds(pl.multiple_of((c * 2 + sub) * part, 8), part)

    dlf[...] = dot(decoded, grad_logits, TN)
    dec_pair = {}
    for k in every:
        dsb[k] = dlf[part_rows(chip(k), so)].astype(jnp.bfloat16)
        dec_pair[k] = remote(dsb.at[k], dpr.at[k], core)
        dec_pair[k].start()

    dec_chip = {}
    for k in others:
        dec_pair[k].wait_recv()
        dps[k] = (dlf[part_rows(chip(k), s)] + dpr[k].astype(jnp.float32)).astype(jnp.bfloat16)
        dec_chip[k] = remote(dps.at[k], drr.at[k], {"tok": chip(k)})
        dec_chip[k].start()

    grad_copy.wait_recv()
    act_copy.wait_recv()
    both = jnp.concatenate([gs[...].astype(jnp.float32), gr[...].astype(jnp.float32)], axis=0)
    both_t = both.T
    for i in range(2 * tok_n):
        gat[i] = both_t[i * part : (i + 1) * part].astype(jnp.bfloat16)
    nar_pair = {}
    for k in every:
        gsb[k] = dot(gat[chip(k) * 2 + so], active[...]).astype(jnp.bfloat16)
        nar_pair[k] = remote(gsb.at[k], gpr.at[k], core)
        nar_pair[k].start()
    nar_chip = {}
    for k in others:
        mine = dot(gat[chip(k) * 2 + s], active[...])
        nar_pair[k].wait_recv()
        gps[k] = (mine + gpr[k].astype(jnp.float32)).astype(jnp.bfloat16)
        nar_chip[k] = remote(gps.at[k], grr.at[k], {"tok": chip(k)})
        nar_chip[k].start()
    dec_pair[0].wait_recv()
    dec_sum = dlf[part_rows(t, s)] + dpr[0].astype(jnp.float32)
    for k in others:
        dec_chip[k].wait_recv()
        dec_sum = dec_sum + drr[k].astype(jnp.float32)
    dx[...] = dec_sum
    dec_side = remote(dx, dxr, side)
    dec_side.start()
    nar_pair[0].wait_recv()
    gnar_ref[...] = dot(gat[t * 2 + s], active[...]) + gpr[0].astype(jnp.float32)
    dec_side.wait_recv()
    gdec_ref[...] = dec_sum + dxr[...]
    for k in others:
        nar_chip[k].wait_recv()
        gnar_ref[...] += grr[k].astype(jnp.float32)

    for group in (
        fast_pair,
        fast_chip,
        gather_chip,
        gather_core,
        dec_pair,
        nar_pair,
        dec_chip,
        nar_chip,
    ):
        for copy in group.values():
            copy.wait_send()
    for copy in (
        head_copy,
        act_copy,
        grad_copy,
        dec_side,
        outw_side_in,
        outw_twin,
        outw_core,
        outw_core2,
        wide_side_in,
        wide_twin,
        wide_core,
        wide_core2,
        narrow_side_in,
        narrow_twin,
        narrow_core,
        narrow_core2,
    ):
        copy.wait_send()


def hand_out(*refs):
    count = len(refs) // 2
    for i in range(count):
        refs[count + i][...] = refs[i][...]


def on_device_kernel(
    in_tokens,
    target_views,
    target_rays,
    camera_turn,
    camera_anchor,
    pixels_true,
    transient,
    query_weight,
    key_weight,
    value_weight,
    rate_weight,
    rate_bias,
    fast_init,
    out_weight,
    ray_weight,
    norm_gain,
    wide_weight,
    narrow_weight,
    decode_gain,
    decode_weight,
):
    tok_n = lax.axis_size("tok")
    devices = tok_n * lax.axis_size("sub")
    in_total = in_tokens.shape[0] * devices
    target_total = target_views.shape[0] * devices
    half = pixels_true.shape[2]
    model = in_tokens.shape[1]
    hidden = wide_weight.shape[1]
    width, depth = fast_init.shape[2:]
    fast_rows = -(-(3 * width // devices) // CHUNK_PAD) * CHUNK_PAD
    part = model // devices
    logit_n = decode_weight.shape[1]
    vmem = pl.BlockSpec(memory_space=pltpu.VMEM)
    anywhere = pl.BlockSpec(memory_space=pl.ANY)
    bf16, f32 = jnp.bfloat16, jnp.float32
    fast_buf = pltpu.VMEM((tok_n, fast_rows, depth), bf16)
    row_buf = pltpu.VMEM((half, model), bf16)
    dec_buf = pltpu.VMEM((tok_n, part, logit_n), bf16)
    nar_buf = pltpu.VMEM((tok_n, part, hidden), bf16)
    copies = 4 * tok_n + 4 * (tok_n - 1) + 16
    render, grad_decode, grad_narrow = pl.pallas_call(
        functools.partial(
            scene_kernel,
            tok_n,
            RATE_SCALE / math.sqrt(in_total),
            1.0 / (transient.shape[-1] * math.sqrt(target_total)),
        ),
        out_shape=(
            jax.ShapeDtypeStruct((half, pixels_true.shape[3]), bf16),
            jax.ShapeDtypeStruct((part, logit_n), f32),
            jax.ShapeDtypeStruct((part, hidden), f32),
        ),
        in_specs=[pl.BlockSpec(memory_space=pltpu.SMEM)] + [vmem] * 9 + [anywhere] * 10,
        out_specs=(vmem, vmem, vmem),
        scratch_shapes=[
            pltpu.VMEM(in_tokens.shape, bf16),
            pltpu.VMEM((width, model), bf16),
            pltpu.VMEM((width, model), bf16),
            pltpu.VMEM((3, width, depth), bf16),
            pltpu.VMEM(ray_weight.shape, bf16),
            pltpu.VMEM((width, model), bf16),
            pltpu.VMEM((2, half, model), bf16),
            pltpu.VMEM((2, half, width), bf16),
            pltpu.VMEM(out_weight.shape, bf16),
            pltpu.VMEM(wide_weight.shape, bf16),
            pltpu.VMEM(narrow_weight.shape, bf16),
            pltpu.VMEM((half, hidden), bf16),
            pltpu.VMEM(out_weight.shape, bf16),
            pltpu.VMEM(wide_weight.shape, bf16),
            pltpu.VMEM(narrow_weight.shape, bf16),
            pltpu.VMEM(decode_weight.shape, bf16),
            pltpu.VMEM((3 * width, depth), f32),
            pltpu.VMEM((3 * width, depth), f32),
        ]
        + [fast_buf] * 6
        + [pltpu.VMEM((half, width), bf16)] * 2
        + [row_buf] * 2
        + [
            pltpu.VMEM((2 * half, hidden), bf16),
            pltpu.VMEM((devices, part, 2 * half), bf16),
            pltpu.VMEM((model, logit_n), f32),
        ]
        + [dec_buf] * 4
        + [pltpu.VMEM((part, logit_n), f32)] * 2
        + [nar_buf] * 4
        + [
            pltpu.SemaphoreType.DMA((copies,)),
            pltpu.SemaphoreType.DMA((copies,)),
            pltpu.SemaphoreType.DMA((9 + in_tokens.shape[0] // 512,)),
        ],
        compiler_params=pltpu.CompilerParams(
            collective_id=0, has_side_effects=True, vmem_limit_bytes=60 * 2**20
        ),
    )(
        rate_bias,
        target_views,
        target_rays,
        camera_turn.T,
        camera_anchor.T,
        rate_weight.T,
        pixels_true[0, 0],
        transient[0, 0].T,
        norm_gain,
        decode_gain,
        in_tokens,
        key_weight.T,
        value_weight.T,
        fast_init[0],
        ray_weight,
        query_weight.T,
        out_weight,
        wide_weight,
        narrow_weight,
        decode_weight,
    )
    render, grad_decode, grad_narrow = pl.pallas_call(
        hand_out,
        out_shape=tuple(
            jax.ShapeDtypeStruct(v.shape, v.dtype) for v in (render, grad_decode, grad_narrow)
        ),
        in_specs=[vmem] * 3,
        out_specs=(vmem,) * 3,
    )(render, grad_decode, grad_narrow)
    return (render[None, None], grad_decode, grad_narrow)


def kernel_fits(mesh):
    return mesh.shape["groups"] == 2 and mesh.shape["head"] == 2 and (
        mesh.shape["sub"] == 2 and mesh.shape["tok"] in (2, 4)
    )


def solution(mesh):
    in_specs = (
        P(("groups", "tok", "sub"), None),
        P(("groups", "tok", "sub")),
        P(("groups", "tok", "sub")),
        P("groups", None),
        P("groups", None),
        P(("groups", "tok", "sub"), "head", None, None),
        P(("groups", "tok", "sub"), "head", None, None),
        P(None, "head"),
        P(None, "head"),
        P(None, "head"),
        P(None, "head"),
        P("head"),
        P("head", None, None, None),
        P("head", None),
        P(),
        P(),
        P(None, "head"),
        P(None, "head"),
        P(),
        P(),
    )
    out_specs = (
        P(("groups", "tok", "sub"), "head", None, None),
        P(("groups", "tok", "sub"), None),
        P(("groups", "tok", "sub"), "head"),
    )
    body = on_device_kernel if kernel_fits(mesh) else on_device
    return jax.shard_map(
        body, mesh=mesh, in_specs=in_specs, out_specs=out_specs, check_vma=False
    )
```
